256 devices in a mesh: lat: 8 (over y_hi, x), lon: 32 (over y_lo, z, core).
Axes of the slice: x: 4, y: 4 (y_hi: 2, y_lo: 2; y = y_hi * 2 + y_lo), z: 8, core: 2. Of those that a mesh axis runs over, the one named last changes fastest.
Arguments:
- state: bfloat16 [128, 128, 4096], P(None, 'lat', 'lon'), may hold values from -6 to 6
- heat_cot: bfloat16 [128, 128, 4096], P(None, 'lat', 'lon'), may hold values from -6 to 6
- state_cot: float32 [128, 128, 4096], P(None, 'lat', 'lon'), may hold values from -6 to 6
- courant_lon: bfloat16 [128, 128, 4096], P(None, 'lat', 'lon'), may hold values from -0.29882812 to 0.29882812
- courant_lat: bfloat16 [128, 128, 4096], P(None, 'lat', 'lon'), may hold values from -0.29882812 to 0.29882812
- w_first: bfloat16 [512, 128], replicated, may hold values from -0.5 to 0.5
- w_second: bfloat16 [512, 512], replicated, may hold values from -0.25 to 0.25
- w_third: bfloat16 [128, 512], replicated, may hold values from -0.25 to 0.25
Outputs:
- state_grad: float32 [128, 128, 4096], P(None, 'lat', 'lon')
- grad_first: float32 [512, 128], replicated
- grad_second: float32 [512, 512], replicated
- grad_third: float32 [128, 512], replicated
The draws below stay inside these ranges and needn't reach their ends.
All inputs are finite; a program needn't handle non-finite values.
Results may differ from the reference program's by a relative error of at most 0.006.
Values may be sent and summed in bfloat16 or wider, within the bound.
A program may use at most 128 MiB of HBM per device.

```python
import math
import jax
import jax.numpy as jnp
from jax import lax

LEV = 128
HID = 512
SUBSTEPS = 3
CLAT = 16
NLAT = 128
NLON = 4096
N_LAT = 8


def shard_levels(stream_key, shape, shards, smallest, high):
    factor_of = 1.0
    for axis_at, shards_of in shards:
        steps = jax.random.uniform(jax.random.fold_in(jax.random.fold_in(stream_key, 6), axis_at), (shards_of,), jnp.float32, smallest / len(shards), high / len(shards))
        factor_of = factor_of * jnp.repeat(jnp.exp(steps), shape[axis_at] // shards_of).reshape((-1,) + (1,) * (len(shape) - 1 - axis_at))
    return factor_of


def gaussian(stream_key, dims, deviation, limit, shards=(), kind=jnp.bfloat16):
    result = deviation * jax.random.normal(stream_key, dims, jnp.float32)
    if shards:
        result = result * shard_levels(stream_key, dims, shards, -0.22, 0.18)
    return jnp.clip(result, -limit, limit).astype(kind)


def setup_inputs(seed: int = 0) -> dict:
    seeds = jax.random.split(jax.random.key(seed), 9)
    state = gaussian(seeds[0], (LEV, NLAT, NLON), 1.0, 6.0, ((1, 8), (2, 32)))
    heat_cot = gaussian(seeds[1], (LEV, NLAT, NLON), 1.0, 6.0, ((1, 8), (2, 32)))
    state_cot = gaussian(seeds[2], (LEV, NLAT, NLON), 1.0, 6.0, ((1, 8), (2, 32)), jnp.float32)
    courant_lon = jnp.clip(jax.random.uniform(seeds[3], (LEV, NLAT, NLON), jnp.float32, -0.29882812, 0.29882812) * shard_levels(seeds[3], (LEV, NLAT, NLON), ((1, 8), (2, 32)), -0.4, 0.0), -0.29882812, 0.29882812).astype(jnp.bfloat16)
    courant_lat = jnp.clip(jax.random.uniform(seeds[4], (LEV, NLAT, NLON), jnp.float32, -0.29882812, 0.29882812) * shard_levels(seeds[4], (LEV, NLAT, NLON), ((1, 8), (2, 32)), -0.4, 0.0), -0.29882812, 0.29882812).astype(jnp.bfloat16)
    w_first = gaussian(seeds[5], (HID, LEV), LEV ** -0.5, 0.5)
    w_second = gaussian(seeds[6], (HID, HID), HID ** -0.5, 0.25)
    w_third = gaussian(seeds[7], (LEV, HID), HID ** -0.5, 0.25)
    return dict(state=state, heat_cot=heat_cot, state_cot=state_cot, courant_lon=courant_lon, courant_lat=courant_lat, w_first=w_first, w_second=w_second, w_third=w_third)


EPSILON = 1e-05

def silu_slope(pre):
    sigma = jax.nn.sigmoid(pre)
    return sigma * (1.0 + pre * (1.0 - sigma))

def contract_first(left, right):
    return lax.dot_general(left, right, (((0,), (0,)), ((), ())), preferred_element_type=jnp.float32)

def contract_last(left, right):
    return lax.dot_general(left, right, (((1,), (1,)), ((), ())), preferred_element_type=jnp.float32)

def mlp_backward(column_state, column_cot, w_first, w_second, w_third):
    values = column_state.astype(jnp.float32)
    inverse = lax.rsqrt(lax.optimization_barrier(jnp.mean(values * values, axis=0, keepdims=True)) + EPSILON)
    normed = values * inverse
    inputs = normed.astype(jnp.bfloat16)
    pre_first = jnp.dot(w_first, inputs, preferred_element_type=jnp.float32)
    act_first = jax.nn.silu(pre_first).astype(jnp.bfloat16)
    pre_second = jnp.dot(w_second, act_first, preferred_element_type=jnp.float32)
    act_second = jax.nn.silu(pre_second).astype(jnp.bfloat16)
    grad_third = contract_last(column_cot, act_second)
    back_second = (contract_first(w_third, column_cot) * silu_slope(pre_second)).astype(jnp.bfloat16)
    grad_second = contract_last(back_second, act_first)
    back_first = (contract_first(w_second, back_second) * silu_slope(pre_first)).astype(jnp.bfloat16)
    grad_first = contract_last(back_first, inputs)
    input_cot = contract_first(w_first, back_first)
    state_part = inverse * (input_cot - normed * lax.optimization_barrier(jnp.mean(input_cot * normed, axis=0, keepdims=True)))
    return (state_part, grad_first, grad_second, grad_third)

def pad_field(field):
    padded = jnp.pad(field, ((0, 0), (1, 1), (0, 0)))
    return jnp.pad(padded, ((0, 0), (0, 0), (1, 1)), mode='wrap')

def adjoint_step(padded, lon_faces, lat_faces):
    centre = padded[:, 1:-1, 1:-1]
    rows_mid = padded[:, 1:-1, :]
    lon_diff = rows_mid[:, :, 1:] - rows_mid[:, :, :-1]
    east_term = jnp.maximum(lon_faces[:, 1:-1, 1:-1], 0.0) * lon_diff[:, :, 1:]
    west_term = jnp.minimum(lon_faces[:, 1:-1, :-2], 0.0) * lon_diff[:, :, :-1]
    cols_mid = padded[:, :, 1:-1]
    lat_diff = cols_mid[:, 1:, :] - cols_mid[:, :-1, :]
    north_term = jnp.maximum(lat_faces[:, 1:-1, 1:-1], 0.0) * lat_diff[:, 1:, :]
    south_term = jnp.minimum(lat_faces[:, :-2, 1:-1], 0.0) * lat_diff[:, :-1, :]
    return centre + east_term + west_term + north_term + south_term

def reference(state, heat_cot, state_cot, courant_lon, courant_lat, w_first, w_second, w_third):

    def one_block(carry, index):
        start = (index * CLAT).astype(jnp.int32)
        block_state = lax.dynamic_slice_in_dim(state, start, CLAT, 1).reshape(LEV, CLAT * NLON)
        block_cot = lax.dynamic_slice_in_dim(heat_cot, start, CLAT, 1).reshape(LEV, CLAT * NLON)
        part, first, second, third = mlp_backward(block_state, block_cot, w_first, w_second, w_third)
        return ((carry[0] + first, carry[1] + second, carry[2] + third), part.reshape(LEV, CLAT, NLON))
    init = (jnp.zeros((HID, LEV), jnp.float32), jnp.zeros((HID, HID), jnp.float32), jnp.zeros((LEV, HID), jnp.float32))
    sums, parts = lax.scan(one_block, init, jnp.arange(N_LAT, dtype=jnp.int32))
    state_part = parts.transpose(1, 0, 2, 3).reshape(LEV, NLAT, NLON)
    cotangent = state_cot + state_part
    lon_pad = pad_field(courant_lon.astype(jnp.float32))
    lat_pad = pad_field(courant_lat.astype(jnp.float32))
    for substep in range(SUBSTEPS):
        cotangent = adjoint_step(pad_field(cotangent), lon_pad, lat_pad)
    grad_scale = 1.0 / math.sqrt(NLAT * NLON)
    return (cotangent, sums[0] * grad_scale, sums[1] * grad_scale, sums[2] * grad_scale)
```

```python
import functools
import math

import jax
import jax.numpy as jnp
from jax import lax
from jax.experimental import pallas as pl
from jax.experimental.pallas import tpu as pltpu
from jax.sharding import PartitionSpec as P

EPSILON = 1e-05
SUBSTEPS = 3
MESH = pl.DeviceIdType.MESH
BF = jnp.bfloat16
F32 = jnp.float32
LEV = 128
HID = 512
ROWS = 16
LON = 128
COLS = ROWS * LON
CHUNK_ROWS = 4
CHUNK = CHUNK_ROWS * LON
CHUNKS = ROWS // CHUNK_ROWS
PLANE = 16
DEPTH = 8
ROUNDS = ((4, 1, False), (0, 4, True), (5, 1, False))
FINISH_ROWS = 512


def dot(a, b):
    return jnp.dot(a, b, preferred_element_type=F32)


def dot_last(a, b):
    return lax.dot_general(a, b, (((1,), (1,)), ((), ())), preferred_element_type=F32)


def silu_and_slope(pre):
    sigma = 0.5 * jnp.tanh(0.5 * pre) + 0.5
    act = pre * sigma
    return act, sigma + act * (1.0 - sigma)


def place():
    lat, lon = lax.axis_index("lat"), lax.axis_index("lon")
    core = lax.rem(lon, 2)
    depth = lax.rem(lax.div(lon, 2), DEPTH)
    plane = lat * 2 + lax.div(lon, 16)
    return lat, lon, core, depth, plane


def loop(lo, hi, body):
    lax.fori_loop(lo, hi, lambda k, carry: (body(k), carry)[1], 0)


class Reduction:
    def __init__(self, part, plane_first, bufs, sems):
        self.part = part
        self.send0, self.recv0, self.half, self.send1, self.recv1, self.recv2, self.full = bufs
        (self.s0, self.r0, self.s1, self.r1, self.s2, self.r2, self.s3, self.r3, self.s4, self.r4) = sems
        lat, lon, self.core, depth, plane = place()
        self.sibling = (lat, lon + 1 - 2 * self.core)
        x, y = lax.rem(lat, 4), lax.div(lat, 4) * 2 + lax.div(lon, 16)
        planes, depths = [], []
        for kx, ky in sorted(((a, b) for a in range(4) for b in range(4) if a or b),
                             key=lambda k: -min(k[0], 4 - k[0]) - min(k[1], 4 - k[1])):
            to_x, to_y = lax.rem(x + kx, 4), lax.rem(y + ky, 4)
            to_lat, to_part = lax.div(to_y, 2) * 4 + to_x, lax.rem(to_y, 2)
            planes.append((to_lat * 2 + to_part, (to_lat, to_part * 16 + lax.rem(lon, 16))))
        for k in sorted(range(1, DEPTH), key=lambda k: -min(k, DEPTH - k)):
            to = lax.rem(depth + k, DEPTH)
            depths.append((to, (lat, lax.div(lon, 16) * 16 + to * 2 + self.core)))
        groups = ((plane, planes), (depth, depths))
        (self.me1, self.peers1), (self.me2, self.peers2) = groups if plane_first else groups[::-1]
        self.across = 4 if plane_first else 2

    def piece(self, index, base=0):
        width = HID // self.across
        row = pl.multiple_of(base + lax.div(index, self.across) * 16, 16)
        lane = pl.multiple_of(lax.rem(index, self.across) * width, width)
        return (slice(None), pl.ds(row, 16), pl.ds(lane, width))

    def copy0(self):
        return pltpu.make_async_remote_copy(
            src_ref=self.send0, dst_ref=self.recv0, send_sem=self.s0, recv_sem=self.r0,
            device_id=self.sibling, device_id_type=MESH)

    def copies1(self):
        return [pltpu.make_async_remote_copy(
            src_ref=self.send1.at[self.piece(to)], dst_ref=self.recv1.at[n],
            send_sem=self.s1.at[n], recv_sem=self.r1.at[n],
            device_id=device, device_id_type=MESH) for n, (to, device) in enumerate(self.peers1)]

    def copies2(self):
        mine = self.recv2.at[self.me2]
        return [pltpu.make_async_remote_copy(
            src_ref=mine, dst_ref=mine, send_sem=self.s2.at[n], recv_sem=self.r2.at[n],
            device_id=device, device_id_type=MESH) for n, (_, device) in enumerate(self.peers2)]

    def copies3(self):
        mine = self.full.at[self.piece(self.me1, 64 * self.core)]
        return [pltpu.make_async_remote_copy(
            src_ref=mine, dst_ref=mine, send_sem=self.s3.at[n], recv_sem=self.r3.at[n],
            device_id=device, device_id_type=MESH) for n, (_, device) in enumerate(self.peers1)]

    def copy4(self):
        mine = self.full.at[:, pl.ds(pl.multiple_of(64 * self.core, 64), 64), :]
        return pltpu.make_async_remote_copy(
            src_ref=mine, dst_ref=mine, send_sem=self.s4, recv_sem=self.r4,
            device_id=self.sibling, device_id_type=MESH)

    def step0(self):
        other = pl.multiple_of(64 * (1 - self.core), 64)
        self.send0[...] = self.part[:, pl.ds(other, 64), :].astype(BF)
        self.copy0().start()

    def step1(self):
        self.copy0().wait()
        mine = pl.multiple_of(64 * self.core, 64)
        self.half[...] = self.part[:, pl.ds(mine, 64), :] + self.recv0[...].astype(F32)
        self.send1[...] = self.half[...].astype(BF)
        for copy in self.copies1():
            copy.start()

    def step2(self):
        for copy in self.copies1():
            copy.wait()
        total = self.half[self.piece(self.me1)]
        for n in range(len(self.peers1)):
            total = total + self.recv1[n].astype(F32)
        self.recv2[self.me2] = total.astype(BF)
        for copy in self.copies2():
            copy.start()

    def step3(self):
        for copy in self.copies2():
            copy.wait()
        total = self.recv2[0].astype(F32)
        for n in range(1, len(self.peers2) + 1):
            total = total + self.recv2[n].astype(F32)
        self.full[self.piece(self.me1, 64 * self.core)] = total.astype(BF)
        for copy in self.copies3():
            copy.start()

    def step4(self):
        for copy in self.copies3():
            copy.wait()
        self.copy4().start()

    def finish(self):
        self.copy4().wait()


def kernel(scale, rounds, state_hbm, heat_hbm, scot_hbm, clon_hbm, clat_hbm, w1_hbm, w2_hbm, w3_hbm,
           out_hbm, first_hbm, second_hbm, third_hbm,
           nat_a, nat_b, state, heat, scot, clon, clat, w1, w2, w3, w1t, w2t, w3t,
           normed_s, inv_s, inputs_s, act1_s, slope1_s, back2_s, act2_s, part,
           cot_a, cot_b, high_s, low_s, sides_s, east_f, west_f, north_f, south_f, ends_f,
           shift_m, ends_m, pack_m, out_nat, first, second, third,
           rim_send, rim_recv, row_send, row_recv,
           load_sem, store_sem, rim_ss, rim_rs, row_ss, row_rs,
           *rest):
    lat, lon, core, depth, plane = place()
    lats, lons = lax.axis_size("lat"), lax.axis_size("lon")
    west_id = (lat, lax.rem(lon + lons - 1, lons))
    east_id = (lat, lax.rem(lon + 1, lons))
    up, down = lat < lats - 1, lat > 0
    reds = []
    for n, (lo, count, plane_first) in enumerate(rounds):
        own = rest[17 * n:17 * (n + 1)]
        reds.append(Reduction(part.at[pl.ds(lo, count)], plane_first, own[:7], own[7:]))
    early = reds[:-1]

    barrier = pltpu.get_barrier_semaphore()

    def greet(device):
        pl.semaphore_signal(barrier, inc=1, device_id=device, device_id_type=MESH)

    for _, device in reds[0].peers1 + reds[0].peers2:
        greet(device)
    greet(reds[0].sibling)
    greet(west_id)
    greet(east_id)

    loads = [pltpu.make_async_copy(src, dst, load_sem.at[i]) for i, (src, dst) in
             enumerate(((state_hbm, state), (w1_hbm, w1), (w2_hbm, w2), (w3_hbm, w3), (heat_hbm, heat),
                        (clon_hbm, clon), (clat_hbm, clat), (scot_hbm, scot)))]
    for load in loads:
        load.start()

    down_i = lax.broadcasted_iota(jnp.int32, (LEV, LON), 0)
    lane = lax.broadcasted_iota(jnp.int32, (LEV, LON), 1)
    for half in range(2):
        shift_m[half * LON:(half + 1) * LON, :LON] = (down_i == lane + 1).astype(BF)
        shift_m[half * LON:(half + 1) * LON, LON:] = (down_i + 1 == lane).astype(BF)
    for row in range(ROWS):
        cols = slice(row * LON, (row + 1) * LON)
        ends_m[:LON, cols] = jnp.where((down_i == 2 * row) & (lane == 0), 1.0, 0.0).astype(BF)
        ends_m[LON:, cols] = jnp.where(
            (down_i == 2 * row + 1) & (lane == LON - 1), 1.0, 0.0).astype(BF)
        pack_m[cols, :] = jnp.where(
            ((down_i == LON - 1) & (lane == 2 * row)) | ((down_i == 0) & (lane == 2 * row + 1)),
            1.0, 0.0).astype(BF)
    cot_a[0] = jnp.zeros((LEV, LON), F32)
    cot_b[0] = jnp.zeros((LEV, LON), F32)
    cot_a[ROWS + 1] = jnp.zeros((LEV, LON), F32)
    cot_b[ROWS + 1] = jnp.zeros((LEV, LON), F32)

    @pl.when(jnp.logical_not(down))
    def _():
        for slot in range(SUBSTEPS + 1):
            row_recv[slot, 0] = jnp.zeros((LEV, LON), BF)

    @pl.when(jnp.logical_not(up))
    def _():
        for slot in range(SUBSTEPS):
            row_recv[slot, 1] = jnp.zeros((LEV, LON), BF)

    for load in loads[:5]:
        load.wait()
    nat_a[...] = state[...].astype(F32)
    nat_b[...] = heat[...].astype(F32)
    w1t[...] = w1[...].T
    w2t[...] = w2[...].T
    w3t[...] = w3[...].T

    def rows_of(ref, first):
        return jnp.concatenate(
            [ref[pl.ds(first + i, LEV, stride=ROWS), :] for i in range(CHUNK_ROWS)], axis=1)

    blocks = [slice(128 * m, 128 * (m + 1)) for m in range(4)]

    def add_blocks(index, terms, new):
        for m in blocks:
            part[index, :, m] = terms[m, :] if new else part[index, :, m] + terms[m, :]

    def forward(chunk):
        cols = slice(chunk * CHUNK, (chunk + 1) * CHUNK)
        values = rows_of(nat_a, chunk * CHUNK_ROWS)
        inverse = lax.rsqrt(jnp.mean(values * values, axis=0, keepdims=True) + EPSILON)
        normed = values * inverse
        inputs = normed.astype(BF)
        normed_s[:, cols] = normed
        inv_s[:, cols] = inverse
        inputs_s[:, cols] = inputs
        cot = rows_of(nat_b, chunk * CHUNK_ROWS).astype(BF)
        act, slope = silu_and_slope(dot(w1[...], inputs))
        act1_s[:, cols] = act.astype(BF)
        slope1_s[:, cols] = slope
        act, slope = silu_and_slope(dot(w2[...], act1_s[:, cols]))
        act2_s[chunk % 2] = act.astype(BF)
        back2_s[:, cols] = (dot(w3t[...], cot) * slope).astype(BF)
        add_blocks(4, dot_last(act2_s[chunk % 2], cot), chunk == 0)
        terms = dot_last(back2_s[:, cols], act1_s[:, cols]).reshape(4, 128, HID)
        part[:4] = terms if chunk == 0 else part[:4] + terms

    for chunk in range(CHUNKS):
        forward(chunk)
    pl.semaphore_wait(barrier, (PLANE - 1) + (DEPTH - 1) + 3)
    for red in early:
        red.step0()

    def rim_copy(slot, way):
        return pltpu.make_async_remote_copy(
            src_ref=rim_send.at[slot], dst_ref=rim_recv.at[slot, way],
            send_sem=rim_ss.at[slot, way], recv_sem=rim_rs.at[slot, way],
            device_id=(east_id, west_id)[way], device_id_type=MESH)

    def row_copy(slot, way):
        return pltpu.make_async_remote_copy(
            src_ref=row_send.at[slot, way], dst_ref=row_recv.at[slot, way],
            send_sem=row_ss.at[slot, way], recv_sem=row_rs.at[slot, way],
            device_id=(jnp.clip(lat + (1, -1)[way], 0, lats - 1), lon), device_id_type=MESH)

    def send_rows(slot, ways):
        for way in ways:
            pl.when((up, down)[way])(lambda: row_copy(slot, way).start())

    def wait_rows(slot, ways):
        for way in ways:
            pl.when((up, down)[way])(lambda: row_copy(slot, way).wait_send())
            pl.when((down, up)[way])(lambda: row_copy(slot, way).wait_recv())

    def backward(chunk):
        cols = slice(chunk * CHUNK, (chunk + 1) * CHUNK)
        back = (dot(w2t[...], back2_s[:, cols]) * slope1_s[:, cols]).astype(BF)
        act2_s[chunk % 2] = back
        add_blocks(5, dot_last(back, inputs_s[:, cols]), chunk == 0)
        input_cot = dot(w1t[...], act2_s[chunk % 2])
        normed = normed_s[:, cols]
        state_part = inv_s[:, cols] * (
            input_cot - normed * jnp.mean(input_cot * normed, axis=0, keepdims=True))
        for i in range(CHUNK_ROWS):
            row = chunk * CHUNK_ROWS + i
            keep(row, state_part[:, i * LON:(i + 1) * LON] + scot[pl.ds(row, LEV, stride=ROWS), :],
                 cot_a)

    def keep(row, new, cells):
        cells[row + 1] = new
        high = new.astype(BF)
        high_s[row] = high
        low_s[row] = (new - high.astype(F32)).astype(BF)

    def packed():
        return sum(dot(jnp.concatenate([high_s[row], high_s[row + 1]], axis=1),
                       pack_m[row * LON:(row + 2) * LON, :]) for row in range(0, ROWS, 2)).astype(BF)

    loads[7].wait()
    for chunk in range(CHUNKS // 2):
        backward(chunk)
    for red in early:
        red.step1()
    for chunk in range(CHUNKS // 2, CHUNKS):
        backward(chunk)
    reds[-1].step0()

    def send_halo(slot):
        row_send[slot, 0] = high_s[ROWS - 1]
        row_send[slot, 1] = high_s[0]
        send_rows(slot, (0, 1))
        rim_send[slot] = packed()
        rim_copy(slot, 0).start()
        rim_copy(slot, 1).start()

    loads[5].wait()
    loads[6].wait()
    nat_a[...] = clon[...].astype(F32)
    nat_b[...] = clat[...].astype(F32)
    row_send[SUBSTEPS, 0] = nat_b[pl.ds(ROWS - 1, LEV, stride=ROWS), :].astype(BF)
    send_rows(SUBSTEPS, (0,))
    faces_pairs = [jnp.concatenate(
        [nat_a[pl.ds(row + i, LEV, stride=ROWS), :].astype(BF) for i in range(2)], axis=1)
        for row in range(0, ROWS, 2)]
    rim_send[SUBSTEPS] = sum(dot(pair, pack_m[2 * i * LON:2 * (i + 1) * LON, :])
                             for i, pair in enumerate(faces_pairs)).astype(BF)
    rim_copy(SUBSTEPS, 0).start()
    send_halo(0)
    reds[-1].step1()

    def sides():
        sides_s[...] = dot(jnp.concatenate(
            [high_s[...].reshape(COLS, LON), low_s[...].reshape(COLS, LON)], axis=1), shift_m[...])

    sides()

    def split_lat(row):
        ahead = nat_b[pl.ds(row, LEV, stride=ROWS), :]
        north_f[row] = jnp.maximum(ahead, 0.0)
        south_f[row + 1] = jnp.minimum(ahead, 0.0)

    loop(0, ROWS, split_lat)
    rim_copy(SUBSTEPS, 0).wait()
    wait_rows(SUBSTEPS, (0,))
    south_f[0] = jnp.minimum(row_recv[SUBSTEPS, 0].astype(F32), 0.0)
    west_rim = rim_recv[SUBSTEPS, 0]
    for row in range(ROWS):
        faces = nat_a[pl.ds(row, LEV, stride=ROWS), :]
        west = dot(jnp.concatenate([faces.astype(BF), west_rim], axis=1), jnp.concatenate(
            [shift_m[:LON, LON:], ends_m[:LON, row * LON:(row + 1) * LON]], axis=0))
        west = jnp.minimum(west, 0.0)
        faces = jnp.maximum(faces, 0.0)
        east_f[row] = faces
        west_f[row] = west
        ends_f[row] = jnp.where(lane == LON - 1, faces, jnp.where(lane == 0, -west, 0.0))

    def inner(cells, new_cells):
        def one_row(row):
            centre = cells[row + 1]
            here = pl.ds(pl.multiple_of(row * LEV, LEV), LEV)
            new_cells[row + 1] = (
                centre + east_f[row] * (sides_s[here, :LON] - centre)
                + west_f[row] * (centre - sides_s[here, LON:])
                + north_f[row] * (cells[row + 2] - centre)
                + south_f[row] * (centre - cells[row]))

        loop(0, ROWS, one_row)

    def outer(slot, new_cells, store):
        rim_copy(slot, 0).wait()
        rim_copy(slot, 1).wait()
        wait_rows(slot, (0, 1))
        rims = jnp.concatenate([rim_recv[slot, 0], rim_recv[slot, 1]], axis=1)
        for row in range(0, ROWS, 2):
            ends = dot(rims, ends_m[:, row * LON:(row + 2) * LON])
            for i in range(2):
                new = new_cells[row + i + 1] + ends_f[row + i] * ends[:, i * LON:(i + 1) * LON]
                if row + i == 0:
                    new = new - south_f[0] * row_recv[slot, 0].astype(F32)
                if row + i == ROWS - 1:
                    new = new + north_f[ROWS - 1] * row_recv[slot, 1].astype(F32)
                store(row + i, new, new_cells)

    def into_natural(row, new, cells):
        out_nat[pl.ds(row, LEV, stride=ROWS), :] = new

    stores = [pltpu.make_async_copy(src, dst, store_sem.at[i]) for i, (src, dst) in enumerate(
        ((out_nat, out_hbm), (first, first_hbm), (second, second_hbm), (third, third_hbm)))]

    third_red, second_red, first_red = reds
    inner(cot_a, cot_b)
    third_red.step2()
    second_red.step2()
    outer(0, cot_b, keep)
    send_halo(1)
    first_red.step2()
    sides()
    inner(cot_b, cot_a)
    third_red.step3()
    outer(1, cot_a, keep)
    send_halo(2)
    sides()
    inner(cot_a, cot_b)
    second_red.step3()
    first_red.step3()
    third_red.step4()
    outer(2, cot_b, into_natural)
    stores[0].start()
    first_red.step4()
    second_red.step4()
    third_red.finish()

    def total(index):
        for (lo, count, _), red in zip(rounds, reds):
            if lo <= index < lo + count:
                return red.full[index - lo].astype(F32) * scale

    sum_third = total(4)
    for m in blocks:
        third[:, m] = sum_third[:, m].T
    stores[3].start()
    first_red.finish()
    sum_first = total(5)
    for m in blocks:
        first[m, :] = sum_first[:, m]
    stores[1].start()
    second_red.finish()
    for i, m in enumerate(blocks):
        second[m, :] = total(i)
    stores[2].start()
    for store in stores:
        store.wait()


def reduction_scratch(nb, plane_first):
    n1, n2 = (PLANE, DEPTH) if plane_first else (DEPTH, PLANE)
    width = HID * 4 // n1
    half, piece = (nb, 64, HID), (nb, 16, width)
    bufs = [
        pltpu.VMEM(half, BF), pltpu.VMEM(half, BF), pltpu.VMEM(half, F32), pltpu.VMEM(half, BF),
        pltpu.VMEM((n1 - 1,) + piece, BF), pltpu.VMEM((n2,) + piece, BF), pltpu.VMEM((nb, 128, HID), BF),
    ]
    dma = pltpu.SemaphoreType.DMA
    sems = [dma, dma, dma((n1 - 1,)), dma((n1 - 1,)), dma((n2 - 1,)), dma((n2 - 1,)),
            dma((n1 - 1,)), dma((n1 - 1,)), dma, dma]
    return bufs + sems


def finish_kernel(*refs):
    ins, outs, held, load_sem, store_sem = refs[:4], refs[4:8], refs[8:12], refs[12], refs[13]
    moves = []
    for src, dst, buf in zip(ins, outs, held):
        size = min(src.shape[0], FINISH_ROWS * 128 // src.shape[1])
        for first in range(0, src.shape[0], size):
            rows = pl.ds(first, size)
            n = len(moves)
            moves.append((
                pltpu.make_async_copy(src.at[rows], buf.at[rows], load_sem.at[n]),
                pltpu.make_async_copy(buf.at[rows], dst.at[rows], store_sem.at[n])))
    for load, _ in moves:
        load.start()
    for load, store in moves:
        load.wait()
        store.start()
    for _, store in moves:
        store.wait()


def local(state, heat_cot, state_cot, courant_lon, courant_lat, w_first, w_second, w_third):
    levels, lat_rows, lon_cols = state.shape
    scale = 1.0 / math.sqrt(lat_rows * lon_cols * lax.axis_size("lat") * lax.axis_size("lon"))
    flat = (levels * lat_rows, lon_cols)
    hbm = pl.BlockSpec(memory_space=pl.ANY)
    dma = pltpu.SemaphoreType.DMA
    tile = (LEV, LON)
    bfs = lambda *shapes: [pltpu.VMEM(shape, BF) for shape in shapes]
    f32s = lambda *shapes: [pltpu.VMEM(shape, F32) for shape in shapes]
    grid = (ROWS,) + tile
    halo = (SUBSTEPS + 1, 2)
    scratch = [
        *f32s(flat, flat), *bfs(flat, flat), *f32s(flat), *bfs(flat, flat),
        *bfs((HID, LEV), (HID, HID), (LEV, HID), (LEV, HID), (HID, HID), (HID, LEV)),
        *f32s((LEV, COLS), (1, COLS)), *bfs((LEV, COLS), (HID, COLS)), *f32s((HID, COLS)),
        *bfs((HID, COLS), (2, HID, CHUNK)), *f32s((6, 128, 512)),
        *f32s((ROWS + 2,) + tile, (ROWS + 2,) + tile), *bfs(grid, grid), *f32s((COLS, 2 * LON)),
        *f32s(grid, grid, grid, (ROWS + 1,) + tile, grid),
        *bfs((2 * LON, 2 * LON), (2 * LON, COLS), (COLS, LON)),
        *f32s(flat, (HID, LEV), (HID, HID), (LEV, HID)),
        *bfs((SUBSTEPS + 1,) + tile, halo + tile, halo + tile, halo + tile),
        dma((8,)), dma((4,)), dma(halo), dma(halo), dma(halo), dma(halo),
    ]
    for _, count, plane_first in ROUNDS:
        scratch += reduction_scratch(count, plane_first)
    shapes = (flat, (HID, LEV), (HID, HID), (LEV, HID))
    results = tuple(jax.ShapeDtypeStruct(shape, F32) for shape in shapes)
    out = pl.pallas_call(
        functools.partial(kernel, scale, ROUNDS),
        out_shape=results,
        in_specs=[hbm] * 8,
        out_specs=(hbm,) * 4,
        scratch_shapes=scratch,
        compiler_params=pltpu.CompilerParams(
            collective_id=0, has_side_effects=True, vmem_limit_bytes=60 << 20),
    )(state.reshape(flat), heat_cot.reshape(flat), state_cot.reshape(flat),
      courant_lon.reshape(flat), courant_lat.reshape(flat), w_first, w_second, w_third)
    grid, first, second, third = pl.pallas_call(
        finish_kernel, out_shape=results, in_specs=[hbm] * 4, out_specs=(hbm,) * 4,
        scratch_shapes=[*f32s(*shapes), dma((16,)), dma((16,))],
        compiler_params=pltpu.CompilerParams(vmem_limit_bytes=60 << 20),
    )(*out)
    return grid.reshape(state.shape), first, second, third


def solution(mesh):
    split = P(None, "lat", "lon")
    return jax.shard_map(
        local, mesh=mesh, in_specs=(split,) * 5 + (P(),) * 3,
        out_specs=(split, P(), P(), P()), check_vma=False)
```

```python
import functools
import math

import jax
import jax.numpy as jnp
from jax import lax
from jax.experimental import pallas as pl
from jax.experimental.pallas import tpu as pltpu
from jax.sharding import PartitionSpec as P

EPSILON = 1e-05
SUBSTEPS = 3
MESH = pl.DeviceIdType.MESH
BF = jnp.bfloat16
F32 = jnp.float32
LEV = 128
HID = 512
ROWS = 16
LON = 128
COLS = ROWS * LON
CHUNK_ROWS = 8
CHUNK = CHUNK_ROWS * LON
CHUNKS = ROWS // CHUNK_ROWS
PLANE = 16
DEPTH = 8
ROUNDS = ((0, 2, True), (2, 2, True), (4, 1, False), (5, 1, False))
FINISH_ROWS = 512


def dot(a, b):
    return jnp.dot(a, b, preferred_element_type=F32)


def dot_last(a, b):
    return lax.dot_general(a, b, (((1,), (1,)), ((), ())), preferred_element_type=F32)


def silu_and_slope(pre):
    sigma = 0.5 * jnp.tanh(0.5 * pre) + 0.5
    act = pre * sigma
    return act, sigma + act * (1.0 - sigma)


def place():
    lat, lon = lax.axis_index("lat"), lax.axis_index("lon")
    core = lax.rem(lon, 2)
    depth = lax.rem(lax.div(lon, 2), DEPTH)
    plane = lat * 2 + lax.div(lon, 16)
    return lat, lon, core, depth, plane


def loop(lo, hi, body):
    lax.fori_loop(lo, hi, lambda k, carry: (body(k), carry)[1], 0)


class Reduction:
    def __init__(self, part, plane_first, bufs, sems):
        self.part = part
        self.send0, self.recv0, self.half, self.send1, self.recv1, self.recv2, self.full = bufs
        (self.s0, self.r0, self.s1, self.r1, self.s2, self.r2, self.s3, self.r3, self.s4, self.r4) = sems
        lat, lon, self.core, depth, plane = place()
        self.sibling = (lat, lon + 1 - 2 * self.core)
        x, y = lax.rem(lat, 4), lax.div(lat, 4) * 2 + lax.div(lon, 16)
        planes, depths = [], []
        for kx, ky in sorted(((a, b) for a in range(4) for b in range(4) if a or b),
                             key=lambda k: -min(k[0], 4 - k[0]) - min(k[1], 4 - k[1])):
            to_x, to_y = lax.rem(x + kx, 4), lax.rem(y + ky, 4)
            to_lat, to_part = lax.div(to_y, 2) * 4 + to_x, lax.rem(to_y, 2)
            planes.append((to_lat * 2 + to_part, (to_lat, to_part * 16 + lax.rem(lon, 16))))
        for k in sorted(range(1, DEPTH), key=lambda k: -min(k, DEPTH - k)):
            to = lax.rem(depth + k, DEPTH)
            depths.append((to, (lat, lax.div(lon, 16) * 16 + to * 2 + self.core)))
        groups = ((plane, planes), (depth, depths))
        (self.me1, self.peers1), (self.me2, self.peers2) = groups if plane_first else groups[::-1]
        self.across = 4 if plane_first else 2

    def piece(self, index, base=0):
        width = HID // self.across
        row = pl.multiple_of(base + lax.div(index, self.across) * 16, 16)
        lane = pl.multiple_of(lax.rem(index, self.across) * width, width)
        return (slice(None), pl.ds(row, 16), pl.ds(lane, width))

    def copy0(self):
        return pltpu.make_async_remote_copy(
            src_ref=self.send0, dst_ref=self.recv0, send_sem=self.s0, recv_sem=self.r0,
            device_id=self.sibling, device_id_type=MESH)

    def copies1(self):
        return [pltpu.make_async_remote_copy(
            src_ref=self.send1.at[self.piece(to)], dst_ref=self.recv1.at[n],
            send_sem=self.s1.at[n], recv_sem=self.r1.at[n],
            device_id=device, device_id_type=MESH) for n, (to, device) in enumerate(self.peers1)]

    def copies2(self):
        mine = self.recv2.at[self.me2]
        return [pltpu.make_async_remote_copy(
            src_ref=mine, dst_ref=mine, send_sem=self.s2.at[n], recv_sem=self.r2.at[n],
            device_id=device, device_id_type=MESH) for n, (_, device) in enumerate(self.peers2)]

    def copies3(self):
        mine = self.full.at[self.piece(self.me1, 64 * self.core)]
        return [pltpu.make_async_remote_copy(
            src_ref=mine, dst_ref=mine, send_sem=self.s3.at[n], recv_sem=self.r3.at[n],
            device_id=device, device_id_type=MESH) for n, (_, device) in enumerate(self.peers1)]

    def copy4(self):
        mine = self.full.at[:, pl.ds(pl.multiple_of(64 * self.core, 64), 64), :]
        return pltpu.make_async_remote_copy(
            src_ref=mine, dst_ref=mine, send_sem=self.s4, recv_sem=self.r4,
            device_id=self.sibling, device_id_type=MESH)

    def step0(self):
        other = pl.multiple_of(64 * (1 - self.core), 64)
        self.send0[...] = self.part[:, pl.ds(other, 64), :].astype(BF)
        self.copy0().start()

    def step1(self):
        self.copy0().wait()
        mine = pl.multiple_of(64 * self.core, 64)
        self.half[...] = self.part[:, pl.ds(mine, 64), :] + self.recv0[...].astype(F32)
        self.send1[...] = self.half[...].astype(BF)
        for copy in self.copies1():
            copy.start()

    def step2(self):
        for copy in self.copies1():
            copy.wait()
        total = self.half[self.piece(self.me1)]
        for n in range(len(self.peers1)):
            total = total + self.recv1[n].astype(F32)
        self.recv2[self.me2] = total.astype(BF)
        for copy in self.copies2():
            copy.start()

    def step3(self):
        for copy in self.copies2():
            copy.wait()
        total = self.recv2[0].astype(F32)
        for n in range(1, len(self.peers2) + 1):
            total = total + self.recv2[n].astype(F32)
        self.full[self.piece(self.me1, 64 * self.core)] = total.astype(BF)
        for copy in self.copies3():
            copy.start()

    def step4(self):
        for copy in self.copies3():
            copy.wait()
        self.copy4().start()

    def finish(self):
        self.copy4().wait()


def kernel(scale, rounds, state_hbm, heat_hbm, scot_hbm, clon_hbm, clat_hbm, w1_hbm, w2_hbm, w3_hbm,
           out_hbm, first_hbm, second_hbm, third_hbm,
           nat_a, nat_b, state, heat, scot, clon, clat, w1, w2, w3, w1t, w2t, w3t,
           normed_s, inv_s, inputs_s, act1_s, slope1_s, back2_s, act2_s, back1_s, part,
           cot_a, cot_b, high_s, low_s, sides_s, east_f, west_f, north_f, south_f, ends_f,
           shift_m, ends_m, pack_m, out_nat, first, second, third,
           rim_send, rim_recv, row_send, row_recv,
           load_sem, store_sem, rim_ss, rim_rs, row_ss, row_rs,
           *rest):
    lat, lon, core, depth, plane = place()
    lats, lons = lax.axis_size("lat"), lax.axis_size("lon")
    west_id = (lat, lax.rem(lon + lons - 1, lons))
    east_id = (lat, lax.rem(lon + 1, lons))
    up, down = lat < lats - 1, lat > 0
    reds = []
    for n, (lo, count, plane_first) in enumerate(rounds):
        own = rest[17 * n:17 * (n + 1)]
        reds.append(Reduction(part.at[pl.ds(lo, count)], plane_first, own[:7], own[7:]))
    left_red, right_red, third_red, first_red = reds

    barrier = pltpu.get_barrier_semaphore()

    def greet(device):
        pl.semaphore_signal(barrier, inc=1, device_id=device, device_id_type=MESH)

    for _, device in reds[0].peers1 + reds[0].peers2:
        greet(device)
    greet(reds[0].sibling)
    greet(west_id)
    greet(east_id)

    loads = [pltpu.make_async_copy(src, dst, load_sem.at[i]) for i, (src, dst) in
             enumerate(((state_hbm, state), (w1_hbm, w1), (w2_hbm, w2), (w3_hbm, w3), (heat_hbm, heat),
                        (clon_hbm, clon), (clat_hbm, clat), (scot_hbm, scot)))]
    for load in loads:
        load.start()

    down_i = lax.broadcasted_iota(jnp.int32, (LEV, LON), 0)
    lane = lax.broadcasted_iota(jnp.int32, (LEV, LON), 1)
    for half in range(2):
        shift_m[half * LON:(half + 1) * LON, :LON] = (down_i == lane + 1).astype(BF)
        shift_m[half * LON:(half + 1) * LON, LON:] = (down_i + 1 == lane).astype(BF)
    for row in range(ROWS):
        cols = slice(row * LON, (row + 1) * LON)
        ends_m[:LON, cols] = jnp.where((down_i == 2 * row) & (lane == 0), 1.0, 0.0).astype(BF)
        ends_m[LON:, cols] = jnp.where(
            (down_i == 2 * row + 1) & (lane == LON - 1), 1.0, 0.0).astype(BF)
        pack_m[cols, :] = jnp.where(
            ((down_i == LON - 1) & (lane == 2 * row)) | ((down_i == 0) & (lane == 2 * row + 1)),
            1.0, 0.0).astype(BF)
    cot_a[0] = jnp.zeros((LEV, LON), F32)
    cot_b[0] = jnp.zeros((LEV, LON), F32)
    cot_a[ROWS + 1] = jnp.zeros((LEV, LON), F32)
    cot_b[ROWS + 1] = jnp.zeros((LEV, LON), F32)

    @pl.when(jnp.logical_not(down))
    def _():
        for slot in range(SUBSTEPS + 1):
            row_recv[slot, 0] = jnp.zeros((LEV, LON), BF)

    @pl.when(jnp.logical_not(up))
    def _():
        for slot in range(SUBSTEPS):
            row_recv[slot, 1] = jnp.zeros((LEV, LON), BF)

    for load in loads[:5]:
        load.wait()
    nat_a[...] = state[...].astype(F32)
    nat_b[...] = heat[...].astype(F32)
    w1t[...] = w1[...].T
    w2t[...] = w2[...].T
    w3t[...] = w3[...].T

    def rows_of(ref, first):
        return jnp.concatenate(
            [ref[pl.ds(first + i, LEV, stride=ROWS), :] for i in range(CHUNK_ROWS)], axis=1)

    blocks = [slice(128 * m, 128 * (m + 1)) for m in range(4)]

    halves = [slice(256 * m, 256 * (m + 1)) for m in range(2)]

    def add(here, terms, new):
        part[here] = terms if new else part[here] + terms

    def add_blocks(index, terms, new):
        for m in blocks:
            add((index, slice(None), m), terms[m, :], new)

    def add_second(terms, new):
        for n in range(8):
            side, i, j = n // 4, n // 2 % 2, n % 2
            add((2 * side + i, slice(None), halves[j]), terms[blocks[2 * i + j], halves[side]], new)

    def forward(chunk):
        cols = slice(chunk * CHUNK, (chunk + 1) * CHUNK)
        values = rows_of(nat_a, chunk * CHUNK_ROWS)
        inverse = lax.rsqrt(jnp.mean(values * values, axis=0, keepdims=True) + EPSILON)
        normed = values * inverse
        inputs = normed.astype(BF)
        normed_s[:, cols] = normed
        inv_s[:, cols] = inverse
        inputs_s[:, cols] = inputs
        cot = rows_of(nat_b, chunk * CHUNK_ROWS).astype(BF)
        act, slope = silu_and_slope(dot(w1[...], inputs))
        act1_s[:, cols] = act.astype(BF)
        slope1_s[:, cols] = slope
        act, slope = silu_and_slope(dot(w2[...], act1_s[:, cols]))
        act2_s[:, cols] = act.astype(BF)
        back2_s[:, cols] = (dot(w3t[...], cot) * slope).astype(BF)
        add_blocks(4, dot_last(act2_s[:, cols], cot), chunk == 0)
        add_second(dot_last(back2_s[:, cols], act1_s[:, cols]), chunk == 0)

    for chunk in range(CHUNKS):
        forward(chunk)
    pl.semaphore_wait(barrier, (PLANE - 1) + (DEPTH - 1) + 3)
    left_red.step0()
    right_red.step0()
    third_red.step0()

    def rim_copy(slot, way):
        return pltpu.make_async_remote_copy(
            src_ref=rim_send.at[slot], dst_ref=rim_recv.at[slot, way],
            send_sem=rim_ss.at[slot, way], recv_sem=rim_rs.at[slot, way],
            device_id=(east_id, west_id)[way], device_id_type=MESH)

    def row_copy(slot, way):
        return pltpu.make_async_remote_copy(
            src_ref=row_send.at[slot, way], dst_ref=row_recv.at[slot, way],
            send_sem=row_ss.at[slot, way], recv_sem=row_rs.at[slot, way],
            device_id=(jnp.clip(lat + (1, -1)[way], 0, lats - 1), lon), device_id_type=MESH)

    def send_rows(slot, ways):
        for way in ways:
            pl.when((up, down)[way])(lambda: row_copy(slot, way).start())

    def wait_rows(slot, ways):
        for way in ways:
            pl.when((up, down)[way])(lambda: row_copy(slot, way).wait_send())
            pl.when((down, up)[way])(lambda: row_copy(slot, way).wait_recv())

    def backward(chunk):
        cols = slice(chunk * CHUNK, (chunk + 1) * CHUNK)
        back1_s[:, cols] = (dot(w2t[...], back2_s[:, cols]) * slope1_s[:, cols]).astype(BF)
        add_blocks(5, dot_last(back1_s[:, cols], inputs_s[:, cols]), chunk == 0)

    def input_part(chunk):
        cols = slice(chunk * CHUNK, (chunk + 1) * CHUNK)
        input_cot = dot(w1t[...], back1_s[:, cols])
        normed = normed_s[:, cols]
        state_part = inv_s[:, cols] * (
            input_cot - normed * jnp.mean(input_cot * normed, axis=0, keepdims=True))
        for i in range(CHUNK_ROWS):
            row = chunk * CHUNK_ROWS + i
            keep(row, state_part[:, i * LON:(i + 1) * LON] + scot[pl.ds(row, LEV, stride=ROWS), :],
                 cot_a)

    def keep(row, new, cells):
        cells[row + 1] = new
        high = new.astype(BF)
        high_s[row] = high
        low_s[row] = (new - high.astype(F32)).astype(BF)

    def packed():
        return sum(dot(jnp.concatenate([high_s[row], high_s[row + 1]], axis=1),
                       pack_m[row * LON:(row + 2) * LON, :]) for row in range(0, ROWS, 2)).astype(BF)

    backward(0)
    left_red.step1()
    backward(1)
    right_red.step1()
    third_red.step1()
    first_red.step0()
    loads[7].wait()
    for chunk in range(CHUNKS):
        input_part(chunk)
    first_red.step1()

    def send_halo(slot):
        row_send[slot, 0] = high_s[ROWS - 1]
        row_send[slot, 1] = high_s[0]
        send_rows(slot, (0, 1))
        rim_send[slot] = packed()
        rim_copy(slot, 0).start()
        rim_copy(slot, 1).start()

    loads[5].wait()
    loads[6].wait()
    nat_a[...] = clon[...].astype(F32)
    nat_b[...] = clat[...].astype(F32)
    row_send[SUBSTEPS, 0] = nat_b[pl.ds(ROWS - 1, LEV, stride=ROWS), :].astype(BF)
    send_rows(SUBSTEPS, (0,))
    faces_pairs = [jnp.concatenate(
        [nat_a[pl.ds(row + i, LEV, stride=ROWS), :].astype(BF) for i in range(2)], axis=1)
        for row in range(0, ROWS, 2)]
    rim_send[SUBSTEPS] = sum(dot(pair, pack_m[2 * i * LON:2 * (i + 1) * LON, :])
                             for i, pair in enumerate(faces_pairs)).astype(BF)
    rim_copy(SUBSTEPS, 0).start()
    send_halo(0)

    def sides():
        sides_s[...] = dot(jnp.concatenate(
            [high_s[...].reshape(COLS, LON), low_s[...].reshape(COLS, LON)], axis=1), shift_m[...])

    sides()

    def split_lat(row):
        ahead = nat_b[pl.ds(row, LEV, stride=ROWS), :]
        north_f[row] = jnp.maximum(ahead, 0.0)
        south_f[row + 1] = jnp.minimum(ahead, 0.0)

    loop(0, ROWS, split_lat)
    rim_copy(SUBSTEPS, 0).wait()
    wait_rows(SUBSTEPS, (0,))
    south_f[0] = jnp.minimum(row_recv[SUBSTEPS, 0].astype(F32), 0.0)
    west_rim = rim_recv[SUBSTEPS, 0]
    for row in range(ROWS):
        faces = nat_a[pl.ds(row, LEV, stride=ROWS), :]
        west = dot(jnp.concatenate([faces.astype(BF), west_rim], axis=1), jnp.concatenate(
            [shift_m[:LON, LON:], ends_m[:LON, row * LON:(row + 1) * LON]], axis=0))
        west = jnp.minimum(west, 0.0)
        faces = jnp.maximum(faces, 0.0)
        east_f[row] = faces
        west_f[row] = west
        ends_f[row] = jnp.where(lane == LON - 1, faces, jnp.where(lane == 0, -west, 0.0))

    def inner(cells, new_cells):
        def one_row(row):
            centre = cells[row + 1]
            here = pl.ds(pl.multiple_of(row * LEV, LEV), LEV)
            new_cells[row + 1] = (
                centre + east_f[row] * (sides_s[here, :LON] - centre)
                + west_f[row] * (centre - sides_s[here, LON:])
                + north_f[row] * (cells[row + 2] - centre)
                + south_f[row] * (centre - cells[row]))

        loop(0, ROWS, one_row)

    def outer(slot, new_cells, store):
        rim_copy(slot, 0).wait()
        rim_copy(slot, 1).wait()
        wait_rows(slot, (0, 1))
        rims = jnp.concatenate([rim_recv[slot, 0], rim_recv[slot, 1]], axis=1)
        for row in range(0, ROWS, 2):
            ends = dot(rims, ends_m[:, row * LON:(row + 2) * LON])
            for i in range(2):
                new = new_cells[row + i + 1] + ends_f[row + i] * ends[:, i * LON:(i + 1) * LON]
                if row + i == 0:
                    new = new - south_f[0] * row_recv[slot, 0].astype(F32)
                if row + i == ROWS - 1:
                    new = new + north_f[ROWS - 1] * row_recv[slot, 1].astype(F32)
                store(row + i, new, new_cells)

    def into_natural(row, new, cells):
        out_nat[pl.ds(row, LEV, stride=ROWS), :] = new

    stores = [pltpu.make_async_copy(src, dst, store_sem.at[i]) for i, (src, dst) in enumerate(
        ((out_nat, out_hbm), (first, first_hbm), (second, second_hbm), (third, third_hbm)))]

    inner(cot_a, cot_b)
    third_red.step2()
    left_red.step2()
    right_red.step2()
    outer(0, cot_b, keep)
    send_halo(1)
    first_red.step2()
    sides()
    inner(cot_b, cot_a)
    third_red.step3()
    left_red.step3()
    outer(1, cot_a, keep)
    send_halo(2)
    sides()
    inner(cot_a, cot_b)
    right_red.step3()
    first_red.step3()
    third_red.step4()
    left_red.step4()
    outer(2, cot_b, into_natural)
    stores[0].start()
    third_red.finish()
    for m in blocks:
        third[:, m] = (third_red.full[0, :, m].astype(F32) * scale).T
    stores[3].start()

    def put_second(red, side):
        for i in range(2):
            for j, m in enumerate(halves):
                second[blocks[2 * i + j], side] = red.full[i, :, m].astype(F32) * scale

    right_red.step4()
    first_red.step4()
    left_red.finish()
    put_second(left_red, halves[0])
    right_red.finish()
    put_second(right_red, halves[1])
    stores[2].start()
    first_red.finish()
    for m in blocks:
        first[m, :] = first_red.full[0, :, m].astype(F32) * scale
    stores[1].start()
    for store in stores:
        store.wait()


def reduction_scratch(nb, plane_first):
    n1, n2 = (PLANE, DEPTH) if plane_first else (DEPTH, PLANE)
    width = HID * 4 // n1
    half, piece = (nb, 64, HID), (nb, 16, width)
    bufs = [
        pltpu.VMEM(half, BF), pltpu.VMEM(half, BF), pltpu.VMEM(half, F32), pltpu.VMEM(half, BF),
        pltpu.VMEM((n1 - 1,) + piece, BF), pltpu.VMEM((n2,) + piece, BF), pltpu.VMEM((nb, 128, HID), BF),
    ]
    dma = pltpu.SemaphoreType.DMA
    sems = [dma, dma, dma((n1 - 1,)), dma((n1 - 1,)), dma((n2 - 1,)), dma((n2 - 1,)),
            dma((n1 - 1,)), dma((n1 - 1,)), dma, dma]
    return bufs + sems


def finish_kernel(*refs):
    ins, outs, held, load_sem, store_sem = refs[:4], refs[4:8], refs[8:12], refs[12], refs[13]
    moves = []
    for src, dst, buf in zip(ins, outs, held):
        size = min(src.shape[0], FINISH_ROWS * 128 // src.shape[1])
        for first in range(0, src.shape[0], size):
            rows = pl.ds(first, size)
            n = len(moves)
            moves.append((
                pltpu.make_async_copy(src.at[rows], buf.at[rows], load_sem.at[n]),
                pltpu.make_async_copy(buf.at[rows], dst.at[rows], store_sem.at[n])))
    for load, _ in moves:
        load.start()
    for load, store in moves:
        load.wait()
        store.start()
    for _, store in moves:
        store.wait()


def local(state, heat_cot, state_cot, courant_lon, courant_lat, w_first, w_second, w_third):
    levels, lat_rows, lon_cols = state.shape
    scale = 1.0 / math.sqrt(lat_rows * lon_cols * lax.axis_size("lat") * lax.axis_size("lon"))
    flat = (levels * lat_rows, lon_cols)
    hbm = pl.BlockSpec(memory_space=pl.ANY)
    dma = pltpu.SemaphoreType.DMA
    tile = (LEV, LON)
    bfs = lambda *shapes: [pltpu.VMEM(shape, BF) for shape in shapes]
    f32s = lambda *shapes: [pltpu.VMEM(shape, F32) for shape in shapes]
    grid = (ROWS,) + tile
    halo = (SUBSTEPS + 1, 2)
    scratch = [
        *f32s(flat, flat), *bfs(flat, flat), *f32s(flat), *bfs(flat, flat),
        *bfs((HID, LEV), (HID, HID), (LEV, HID), (LEV, HID), (HID, HID), (HID, LEV)),
        *f32s((LEV, COLS), (1, COLS)), *bfs((LEV, COLS), (HID, COLS)), *f32s((HID, COLS)),
        *bfs((HID, COLS), (HID, COLS), (HID, COLS)), *f32s((6, 128, 512)),
        *f32s((ROWS + 2,) + tile, (ROWS + 2,) + tile), *bfs(grid, grid), *f32s((COLS, 2 * LON)),
        *f32s(grid, grid, grid, (ROWS + 1,) + tile, grid),
        *bfs((2 * LON, 2 * LON), (2 * LON, COLS), (COLS, LON)),
        *f32s(flat, (HID, LEV), (HID, HID), (LEV, HID)),
        *bfs((SUBSTEPS + 1,) + tile, halo + tile, halo + tile, halo + tile),
        dma((8,)), dma((4,)), dma(halo), dma(halo), dma(halo), dma(halo),
    ]
    for _, count, plane_first in ROUNDS:
        scratch += reduction_scratch(count, plane_first)
    shapes = (flat, (HID, LEV), (HID, HID), (LEV, HID))
    results = tuple(jax.ShapeDtypeStruct(shape, F32) for shape in shapes)
    out = pl.pallas_call(
        functools.partial(kernel, scale, ROUNDS),
        out_shape=results,
        in_specs=[hbm] * 8,
        out_specs=(hbm,) * 4,
        scratch_shapes=scratch,
        compiler_params=pltpu.CompilerParams(
            collective_id=0, has_side_effects=True, vmem_limit_bytes=60 << 20),
    )(state.reshape(flat), heat_cot.reshape(flat), state_cot.reshape(flat),
      courant_lon.reshape(flat), courant_lat.reshape(flat), w_first, w_second, w_third)
    grid, first, second, third = pl.pallas_call(
        finish_kernel, out_shape=results, in_specs=[hbm] * 4, out_specs=(hbm,) * 4,
        scratch_shapes=[*f32s(*shapes), dma((16,)), dma((16,))],
        compiler_params=pltpu.CompilerParams(vmem_limit_bytes=60 << 20),
    )(*out)
    return grid.reshape(state.shape), first, second, third


def solution(mesh):
    split = P(None, "lat", "lon")
    return jax.shard_map(
        local, mesh=mesh, in_specs=(split,) * 5 + (P(),) * 3,
        out_specs=(split, P(), P(), P()), check_vma=False)
```

```python
import functools
import math

import jax
import jax.numpy as jnp
from jax import lax
from jax.experimental import pallas as pl
from jax.experimental.pallas import tpu as pltpu
from jax.sharding import PartitionSpec as P

EPSILON = 1e-05
SUBSTEPS = 3
MESH = pl.DeviceIdType.MESH
BF = jnp.bfloat16
F32 = jnp.float32
LEV = 128
HID = 512
ROWS = 16
LON = 128
COLS = ROWS * LON
CHUNK_ROWS = 4
CHUNK = CHUNK_ROWS * LON
CHUNKS = ROWS // CHUNK_ROWS
PLANE = 16
DEPTH = 8
ROUNDS = ((4, 1, False), (0, 4, True), (5, 1, False))
FINISH_ROWS = 512


def dot(a, b):
    return jnp.dot(a, b, preferred_element_type=F32)


def dot_last(a, b):
    return lax.dot_general(a, b, (((1,), (1,)), ((), ())), preferred_element_type=F32)


def silu_and_slope(pre):
    sigma = 0.5 * jnp.tanh(0.5 * pre) + 0.5
    act = pre * sigma
    return act, sigma + act * (1.0 - sigma)


def place():
    lat, lon = lax.axis_index("lat"), lax.axis_index("lon")
    core = lax.rem(lon, 2)
    depth = lax.rem(lax.div(lon, 2), DEPTH)
    plane = lat * 2 + lax.div(lon, 16)
    return lat, lon, core, depth, plane


def loop(lo, hi, body):
    lax.fori_loop(lo, hi, lambda k, carry: (body(k), carry)[1], 0)


class Reduction:
    def __init__(self, part, plane_first, bufs, sems):
        self.part = part
        self.send0, self.recv0, self.half, self.send1, self.recv1, self.recv2, self.full = bufs
        (self.s0, self.r0, self.s1, self.r1, self.s2, self.r2, self.s3, self.r3, self.s4, self.r4) = sems
        lat, lon, self.core, depth, plane = place()
        self.sibling = (lat, lon + 1 - 2 * self.core)
        x, y = lax.rem(lat, 4), lax.div(lat, 4) * 2 + lax.div(lon, 16)
        planes, depths = [], []
        for kx, ky in sorted(((a, b) for a in range(4) for b in range(4) if a or b),
                             key=lambda k: -min(k[0], 4 - k[0]) - min(k[1], 4 - k[1])):
            to_x, to_y = lax.rem(x + kx, 4), lax.rem(y + ky, 4)
            to_lat, to_part = lax.div(to_y, 2) * 4 + to_x, lax.rem(to_y, 2)
            planes.append((to_lat * 2 + to_part, (to_lat, to_part * 16 + lax.rem(lon, 16))))
        for k in sorted(range(1, DEPTH), key=lambda k: -min(k, DEPTH - k)):
            to = lax.rem(depth + k, DEPTH)
            depths.append((to, (lat, lax.div(lon, 16) * 16 + to * 2 + self.core)))
        groups = ((plane, planes), (depth, depths))
        (self.me1, self.peers1), (self.me2, self.peers2) = groups if plane_first else groups[::-1]
        self.across = 4 if plane_first else 2

    def piece(self, index, base=0):
        width = HID // self.across
        row = pl.multiple_of(base + lax.div(index, self.across) * 16, 16)
        lane = pl.multiple_of(lax.rem(index, self.across) * width, width)
        return (slice(None), pl.ds(row, 16), pl.ds(lane, width))

    def copy0(self):
        return pltpu.make_async_remote_copy(
            src_ref=self.send0, dst_ref=self.recv0, send_sem=self.s0, recv_sem=self.r0,
            device_id=self.sibling, device_id_type=MESH)

    def copies1(self):
        return [pltpu.make_async_remote_copy(
            src_ref=self.send1.at[self.piece(to)], dst_ref=self.recv1.at[n],
            send_sem=self.s1, recv_sem=self.r1,
            device_id=device, device_id_type=MESH) for n, (to, device) in enumerate(self.peers1)]

    def copies2(self):
        mine = self.recv2.at[self.me2]
        return [pltpu.make_async_remote_copy(
            src_ref=mine, dst_ref=mine, send_sem=self.s2, recv_sem=self.r2,
            device_id=device, device_id_type=MESH) for _, device in self.peers2]

    def copies3(self):
        mine = self.full.at[self.piece(self.me1, 64 * self.core)]
        return [pltpu.make_async_remote_copy(
            src_ref=mine, dst_ref=mine, send_sem=self.s3, recv_sem=self.r3,
            device_id=device, device_id_type=MESH) for _, device in self.peers1]

    def all_of(self, ref, send_sem, recv_sem):
        return pltpu.make_async_remote_copy(
            src_ref=ref, dst_ref=ref, send_sem=send_sem, recv_sem=recv_sem,
            device_id=self.sibling, device_id_type=MESH)

    def copy4(self):
        mine = self.full.at[:, pl.ds(pl.multiple_of(64 * self.core, 64), 64), :]
        return pltpu.make_async_remote_copy(
            src_ref=mine, dst_ref=mine, send_sem=self.s4, recv_sem=self.r4,
            device_id=self.sibling, device_id_type=MESH)

    def step0(self):
        other = pl.multiple_of(64 * (1 - self.core), 64)
        self.send0[...] = self.part[:, pl.ds(other, 64), :].astype(BF)
        self.copy0().start()

    def step1(self):
        self.copy0().wait()
        mine = pl.multiple_of(64 * self.core, 64)
        self.half[...] = self.part[:, pl.ds(mine, 64), :] + self.recv0[...].astype(F32)
        self.send1[...] = self.half[...].astype(BF)
        for copy in self.copies1():
            copy.start()

    def step2(self):
        self.all_of(self.recv1, self.s1, self.r1).wait()
        total = self.half[self.piece(self.me1)]
        for n in range(len(self.peers1)):
            total = total + self.recv1[n].astype(F32)
        self.recv2[self.me2] = total.astype(BF)
        for copy in self.copies2():
            copy.start()

    def step3(self):
        self.all_of(self.recv2.at[pl.ds(0, len(self.peers2))], self.s2, self.r2).wait()
        total = self.recv2[0].astype(F32)
        for n in range(1, len(self.peers2) + 1):
            total = total + self.recv2[n].astype(F32)
        self.full[self.piece(self.me1, 64 * self.core)] = total.astype(BF)
        for copy in self.copies3():
            copy.start()

    def step4(self):
        self.all_of(self.recv1, self.s3, self.r3).wait()
        self.copy4().start()

    def finish(self):
        self.copy4().wait()


def kernel(scale, rounds, state_hbm, heat_hbm, scot_hbm, clon_hbm, clat_hbm, w1_hbm, w2_hbm, w3_hbm,
           out_hbm, first_hbm, second_hbm, third_hbm,
           nat_a, nat_b, state, heat, scot, clon, clat, w1, w2, w3, w1t, w2t, w3t,
           normed_s, inv_s, inputs_s, act1_s, slope1_s, back2_s, act2_s, part,
           cot_a, cot_b, high_s, low_s, sides_s, east_f, west_f, north_f, south_f, ends_f,
           shift_m, ends_m, pack_m, out_nat, first, second, third,
           rim_send, rim_recv, row_send, row_recv,
           load_sem, store_sem, rim_ss, rim_rs, row_ss, row_rs,
           *rest):
    lat, lon, core, depth, plane = place()
    lats, lons = lax.axis_size("lat"), lax.axis_size("lon")
    west_id = (lat, lax.rem(lon + lons - 1, lons))
    east_id = (lat, lax.rem(lon + 1, lons))
    up, down = lat < lats - 1, lat > 0
    reds = []
    for n, (lo, count, plane_first) in enumerate(rounds):
        own = rest[17 * n:17 * (n + 1)]
        reds.append(Reduction(part.at[pl.ds(lo, count)], plane_first, own[:7], own[7:]))
    early = reds[:-1]

    barrier = pltpu.get_barrier_semaphore()

    def greet(device):
        pl.semaphore_signal(barrier, inc=1, device_id=device, device_id_type=MESH)

    for _, device in reds[0].peers1 + reds[0].peers2:
        greet(device)
    greet(reds[0].sibling)
    greet(west_id)
    greet(east_id)

    loads = [pltpu.make_async_copy(src, dst, load_sem.at[i]) for i, (src, dst) in
             enumerate(((state_hbm, state), (w1_hbm, w1), (w2_hbm, w2), (w3_hbm, w3), (heat_hbm, heat),
                        (clon_hbm, clon), (clat_hbm, clat), (scot_hbm, scot)))]
    for load in loads:
        load.start()

    down_i = lax.broadcasted_iota(jnp.int32, (LEV, LON), 0)
    lane = lax.broadcasted_iota(jnp.int32, (LEV, LON), 1)
    for half in range(2):
        shift_m[half * LON:(half + 1) * LON, :LON] = (down_i == lane + 1).astype(BF)
        shift_m[half * LON:(half + 1) * LON, LON:] = (down_i + 1 == lane).astype(BF)
    for row in range(ROWS):
        cols = slice(row * LON, (row + 1) * LON)
        ends_m[:LON, cols] = jnp.where((down_i == 2 * row) & (lane == 0), 1.0, 0.0).astype(BF)
        ends_m[LON:, cols] = jnp.where(
            (down_i == 2 * row + 1) & (lane == LON - 1), 1.0, 0.0).astype(BF)
        pack_m[cols, :] = jnp.where(
            ((down_i == LON - 1) & (lane == 2 * row)) | ((down_i == 0) & (lane == 2 * row + 1)),
            1.0, 0.0).astype(BF)
    cot_a[0] = jnp.zeros((LEV, LON), F32)
    cot_b[0] = jnp.zeros((LEV, LON), F32)
    cot_a[ROWS + 1] = jnp.zeros((LEV, LON), F32)
    cot_b[ROWS + 1] = jnp.zeros((LEV, LON), F32)

    @pl.when(jnp.logical_not(down))
    def _():
        for slot in range(SUBSTEPS + 1):
            row_recv[slot, 0] = jnp.zeros((LEV, LON), BF)

    @pl.when(jnp.logical_not(up))
    def _():
        for slot in range(SUBSTEPS):
            row_recv[slot, 1] = jnp.zeros((LEV, LON), BF)

    for load in loads[:5]:
        load.wait()
    nat_a[...] = state[...].astype(F32)
    nat_b[...] = heat[...].astype(F32)
    w1t[...] = w1[...].T
    w2t[...] = w2[...].T
    w3t[...] = w3[...].T

    def rows_of(ref, first):
        return jnp.concatenate(
            [ref[pl.ds(first + i, LEV, stride=ROWS), :] for i in range(CHUNK_ROWS)], axis=1)

    blocks = [slice(128 * m, 128 * (m + 1)) for m in range(4)]

    def add_blocks(index, terms, new):
        for m in blocks:
            part[index, :, m] = terms[m, :] if new else part[index, :, m] + terms[m, :]

    def forward(chunk):
        cols = slice(chunk * CHUNK, (chunk + 1) * CHUNK)
        values = rows_of(nat_a, chunk * CHUNK_ROWS)
        inverse = lax.rsqrt(jnp.mean(values * values, axis=0, keepdims=True) + EPSILON)
        normed = values * inverse
        inputs = normed.astype(BF)
        normed_s[:, cols] = normed
        inv_s[:, cols] = inverse
        inputs_s[:, cols] = inputs
        cot = rows_of(nat_b, chunk * CHUNK_ROWS).astype(BF)
        act, slope = silu_and_slope(dot(w1[...], inputs))
        act1_s[:, cols] = act.astype(BF)
        slope1_s[:, cols] = slope
        act, slope = silu_and_slope(dot(w2[...], act1_s[:, cols]))
        act2_s[chunk % 2] = act.astype(BF)
        back2_s[:, cols] = (dot(w3t[...], cot) * slope).astype(BF)
        add_blocks(4, dot_last(act2_s[chunk % 2], cot), chunk == 0)
        terms = dot_last(back2_s[:, cols], act1_s[:, cols]).reshape(4, 128, HID)
        part[:4] = terms if chunk == 0 else part[:4] + terms

    for chunk in range(CHUNKS):
        forward(chunk)
    pl.semaphore_wait(barrier, (PLANE - 1) + (DEPTH - 1) + 3)
    for red in early:
        red.step0()

    def rim_copy(slot, way):
        return pltpu.make_async_remote_copy(
            src_ref=rim_send.at[slot], dst_ref=rim_recv.at[slot, way],
            send_sem=rim_ss.at[slot, way], recv_sem=rim_rs.at[slot, way],
            device_id=(east_id, west_id)[way], device_id_type=MESH)

    def row_copy(slot, way):
        return pltpu.make_async_remote_copy(
            src_ref=row_send.at[slot, way], dst_ref=row_recv.at[slot, way],
            send_sem=row_ss.at[slot, way], recv_sem=row_rs.at[slot, way],
            device_id=(jnp.clip(lat + (1, -1)[way], 0, lats - 1), lon), device_id_type=MESH)

    def send_rows(slot, ways):
        for way in ways:
            pl.when((up, down)[way])(lambda: row_copy(slot, way).start())

    def wait_rows(slot, ways):
        for way in ways:
            pl.when((up, down)[way])(lambda: row_copy(slot, way).wait_send())
            pl.when((down, up)[way])(lambda: row_copy(slot, way).wait_recv())

    def backward(chunk):
        cols = slice(chunk * CHUNK, (chunk + 1) * CHUNK)
        back = (dot(w2t[...], back2_s[:, cols]) * slope1_s[:, cols]).astype(BF)
        act2_s[chunk % 2] = back
        add_blocks(5, dot_last(back, inputs_s[:, cols]), chunk == 0)
        input_cot = dot(w1t[...], act2_s[chunk % 2])
        normed = normed_s[:, cols]
        state_part = inv_s[:, cols] * (
            input_cot - normed * jnp.mean(input_cot * normed, axis=0, keepdims=True))
        for i in range(CHUNK_ROWS):
            row = chunk * CHUNK_ROWS + i
            keep(row, state_part[:, i * LON:(i + 1) * LON] + scot[pl.ds(row, LEV, stride=ROWS), :],
                 cot_a)

    def keep(row, new, cells):
        cells[row + 1] = new
        high = new.astype(BF)
        high_s[row] = high
        low_s[row] = (new - high.astype(F32)).astype(BF)

    def packed():
        return sum(dot(jnp.concatenate([high_s[row], high_s[row + 1]], axis=1),
                       pack_m[row * LON:(row + 2) * LON, :]) for row in range(0, ROWS, 2)).astype(BF)

    loads[7].wait()
    for chunk in range(CHUNKS // 2):
        backward(chunk)
    for red in early:
        red.step1()
    for chunk in range(CHUNKS // 2, CHUNKS):
        backward(chunk)
    reds[-1].step0()

    def send_halo(slot):
        row_send[slot, 0] = high_s[ROWS - 1]
        row_send[slot, 1] = high_s[0]
        send_rows(slot, (0, 1))
        rim_send[slot] = packed()
        rim_copy(slot, 0).start()
        rim_copy(slot, 1).start()

    loads[5].wait()
    loads[6].wait()
    nat_a[...] = clon[...].astype(F32)
    nat_b[...] = clat[...].astype(F32)
    row_send[SUBSTEPS, 0] = nat_b[pl.ds(ROWS - 1, LEV, stride=ROWS), :].astype(BF)
    send_rows(SUBSTEPS, (0,))
    faces_pairs = [jnp.concatenate(
        [nat_a[pl.ds(row + i, LEV, stride=ROWS), :].astype(BF) for i in range(2)], axis=1)
        for row in range(0, ROWS, 2)]
    rim_send[SUBSTEPS] = sum(dot(pair, pack_m[2 * i * LON:2 * (i + 1) * LON, :])
                             for i, pair in enumerate(faces_pairs)).astype(BF)
    rim_copy(SUBSTEPS, 0).start()
    send_halo(0)
    reds[-1].step1()

    def sides():
        sides_s[...] = dot(jnp.concatenate(
            [high_s[...].reshape(COLS, LON), low_s[...].reshape(COLS, LON)], axis=1), shift_m[...])

    sides()

    def split_lat(row):
        ahead = nat_b[pl.ds(row, LEV, stride=ROWS), :]
        north_f[row] = jnp.maximum(ahead, 0.0)
        south_f[row + 1] = jnp.minimum(ahead, 0.0)

    loop(0, ROWS, split_lat)
    rim_copy(SUBSTEPS, 0).wait()
    wait_rows(SUBSTEPS, (0,))
    south_f[0] = jnp.minimum(row_recv[SUBSTEPS, 0].astype(F32), 0.0)
    west_rim = rim_recv[SUBSTEPS, 0]
    for row in range(ROWS):
        faces = nat_a[pl.ds(row, LEV, stride=ROWS), :]
        west = dot(jnp.concatenate([faces.astype(BF), west_rim], axis=1), jnp.concatenate(
            [shift_m[:LON, LON:], ends_m[:LON, row * LON:(row + 1) * LON]], axis=0))
        west = jnp.minimum(west, 0.0)
        faces = jnp.maximum(faces, 0.0)
        east_f[row] = faces
        west_f[row] = west
        ends_f[row] = jnp.where(lane == LON - 1, faces, jnp.where(lane == 0, -west, 0.0))

    def inner(cells, new_cells):
        def one_row(row):
            centre = cells[row + 1]
            here = pl.ds(pl.multiple_of(row * LEV, LEV), LEV)
            new_cells[row + 1] = (
                centre + east_f[row] * (sides_s[here, :LON] - centre)
                + west_f[row] * (centre - sides_s[here, LON:])
                + north_f[row] * (cells[row + 2] - centre)
                + south_f[row] * (centre - cells[row]))

        loop(0, ROWS, one_row)

    def outer(slot, new_cells, store):
        rim_copy(slot, 0).wait()
        rim_copy(slot, 1).wait()
        wait_rows(slot, (0, 1))
        rims = jnp.concatenate([rim_recv[slot, 0], rim_recv[slot, 1]], axis=1)
        for row in range(0, ROWS, 2):
            ends = dot(rims, ends_m[:, row * LON:(row + 2) * LON])
            for i in range(2):
                new = new_cells[row + i + 1] + ends_f[row + i] * ends[:, i * LON:(i + 1) * LON]
                if row + i == 0:
                    new = new - south_f[0] * row_recv[slot, 0].astype(F32)
                if row + i == ROWS - 1:
                    new = new + north_f[ROWS - 1] * row_recv[slot, 1].astype(F32)
                store(row + i, new, new_cells)

    def into_natural(row, new, cells):
        out_nat[pl.ds(row, LEV, stride=ROWS), :] = new

    stores = [pltpu.make_async_copy(src, dst, store_sem.at[i]) for i, (src, dst) in enumerate(
        ((out_nat, out_hbm), (first, first_hbm), (second, second_hbm), (third, third_hbm)))]

    third_red, second_red, first_red = reds
    inner(cot_a, cot_b)
    third_red.step2()
    second_red.step2()
    outer(0, cot_b, keep)
    send_halo(1)
    first_red.step2()
    sides()
    inner(cot_b, cot_a)
    third_red.step3()
    outer(1, cot_a, keep)
    send_halo(2)
    sides()
    inner(cot_a, cot_b)
    second_red.step3()
    first_red.step3()
    third_red.step4()
    outer(2, cot_b, into_natural)
    stores[0].start()
    first_red.step4()
    second_red.step4()
    third_red.finish()

    def total(index):
        for (lo, count, _), red in zip(rounds, reds):
            if lo <= index < lo + count:
                return red.full[index - lo].astype(F32) * scale

    sum_third = total(4)
    for m in blocks:
        third[:, m] = sum_third[:, m].T
    stores[3].start()
    first_red.finish()
    sum_first = total(5)
    for m in blocks:
        first[m, :] = sum_first[:, m]
    stores[1].start()
    second_red.finish()
    for i, m in enumerate(blocks):
        second[m, :] = total(i)
    stores[2].start()
    for store in stores:
        store.wait()


def reduction_scratch(nb, plane_first):
    n1, n2 = (PLANE, DEPTH) if plane_first else (DEPTH, PLANE)
    width = HID * 4 // n1
    half, piece = (nb, 64, HID), (nb, 16, width)
    bufs = [
        pltpu.VMEM(half, BF), pltpu.VMEM(half, BF), pltpu.VMEM(half, F32), pltpu.VMEM(half, BF),
        pltpu.VMEM((n1 - 1,) + piece, BF), pltpu.VMEM((n2,) + piece, BF), pltpu.VMEM((nb, 128, HID), BF),
    ]
    dma = pltpu.SemaphoreType.DMA
    return bufs + [dma] * 10


def finish_kernel(*refs):
    ins, outs, held, load_sem, store_sem = refs[:4], refs[4:8], refs[8:12], refs[12], refs[13]
    moves = []
    for src, dst, buf in zip(ins, outs, held):
        size = min(src.shape[0], FINISH_ROWS * 128 // src.shape[1])
        for first in range(0, src.shape[0], size):
            rows = pl.ds(first, size)
            n = len(moves)
            moves.append((
                pltpu.make_async_copy(src.at[rows], buf.at[rows], load_sem.at[n]),
                pltpu.make_async_copy(buf.at[rows], dst.at[rows], store_sem.at[n])))
    for load, _ in moves:
        load.start()
    for load, store in moves:
        load.wait()
        store.start()
    for _, store in moves:
        store.wait()


def local(state, heat_cot, state_cot, courant_lon, courant_lat, w_first, w_second, w_third):
    levels, lat_rows, lon_cols = state.shape
    scale = 1.0 / math.sqrt(lat_rows * lon_cols * lax.axis_size("lat") * lax.axis_size("lon"))
    flat = (levels * lat_rows, lon_cols)
    hbm = pl.BlockSpec(memory_space=pl.ANY)
    dma = pltpu.SemaphoreType.DMA
    tile = (LEV, LON)
    bfs = lambda *shapes: [pltpu.VMEM(shape, BF) for shape in shapes]
    f32s = lambda *shapes: [pltpu.VMEM(shape, F32) for shape in shapes]
    grid = (ROWS,) + tile
    halo = (SUBSTEPS + 1, 2)
    scratch = [
        *f32s(flat, flat), *bfs(flat, flat), *f32s(flat), *bfs(flat, flat),
        *bfs((HID, LEV), (HID, HID), (LEV, HID), (LEV, HID), (HID, HID), (HID, LEV)),
        *f32s((LEV, COLS), (1, COLS)), *bfs((LEV, COLS), (HID, COLS)), *f32s((HID, COLS)),
        *bfs((HID, COLS), (2, HID, CHUNK)), *f32s((6, 128, 512)),
        *f32s((ROWS + 2,) + tile, (ROWS + 2,) + tile), *bfs(grid, grid), *f32s((COLS, 2 * LON)),
        *f32s(grid, grid, grid, (ROWS + 1,) + tile, grid),
        *bfs((2 * LON, 2 * LON), (2 * LON, COLS), (COLS, LON)),
        *f32s(flat, (HID, LEV), (HID, HID), (LEV, HID)),
        *bfs((SUBSTEPS + 1,) + tile, halo + tile, halo + tile, halo + tile),
        dma((8,)), dma((4,)), dma(halo), dma(halo), dma(halo), dma(halo),
    ]
    for _, count, plane_first in ROUNDS:
        scratch += reduction_scratch(count, plane_first)
    shapes = (flat, (HID, LEV), (HID, HID), (LEV, HID))
    results = tuple(jax.ShapeDtypeStruct(shape, F32) for shape in shapes)
    out = pl.pallas_call(
        functools.partial(kernel, scale, ROUNDS),
        out_shape=results,
        in_specs=[hbm] * 8,
        out_specs=(hbm,) * 4,
        scratch_shapes=scratch,
        compiler_params=pltpu.CompilerParams(
            collective_id=0, has_side_effects=True, vmem_limit_bytes=60 << 20),
    )(state.reshape(flat), heat_cot.reshape(flat), state_cot.reshape(flat),
      courant_lon.reshape(flat), courant_lat.reshape(flat), w_first, w_second, w_third)
    grid, first, second, third = pl.pallas_call(
        finish_kernel, out_shape=results, in_specs=[hbm] * 4, out_specs=(hbm,) * 4,
        scratch_shapes=[*f32s(*shapes), dma((16,)), dma((16,))],
        compiler_params=pltpu.CompilerParams(vmem_limit_bytes=60 << 20),
    )(*out)
    return grid.reshape(state.shape), first, second, third


def solution(mesh):
    split = P(None, "lat", "lon")
    return jax.shard_map(
        local, mesh=mesh, in_specs=(split,) * 5 + (P(),) * 3,
        out_specs=(split, P(), P(), P()), check_vma=False)
```

```python
import functools
import math

import jax
import jax.numpy as jnp
from jax import lax
from jax.experimental import pallas as pl
from jax.experimental.pallas import tpu as pltpu
from jax.sharding import PartitionSpec as P

EPSILON = 1e-05
SUBSTEPS = 3
MESH = pl.DeviceIdType.MESH
BF = jnp.bfloat16
F32 = jnp.float32
LEV = 128
HID = 512
ROWS = 16
LON = 128
COLS = ROWS * LON
CHUNK_ROWS = 4
CHUNK = CHUNK_ROWS * LON
CHUNKS = ROWS // CHUNK_ROWS
PLANE = 16
DEPTH = 8
ROUNDS = ((4, 1, False), (0, 4, True), (5, 1, False))
FINISH_ROWS = 512


def dot(a, b):
    return jnp.dot(a, b, preferred_element_type=F32)


def dot_last(a, b):
    return lax.dot_general(a, b, (((1,), (1,)), ((), ())), preferred_element_type=F32)


def silu_and_slope(pre):
    sigma = 0.5 * jnp.tanh(0.5 * pre) + 0.5
    act = pre * sigma
    return act, sigma + act * (1.0 - sigma)


def place():
    lat, lon = lax.axis_index("lat"), lax.axis_index("lon")
    core = lax.rem(lon, 2)
    depth = lax.rem(lax.div(lon, 2), DEPTH)
    plane = lat * 2 + lax.div(lon, 16)
    return lat, lon, core, depth, plane


def loop(lo, hi, body):
    lax.fori_loop(lo, hi, lambda k, carry: (body(k), carry)[1], 0)


class Reduction:
    def __init__(self, part, plane_first, bufs, sems):
        self.part = part
        self.send0, self.recv0, self.half, self.send1, self.recv1, self.recv2, self.full = bufs
        (self.s0, self.r0, self.s1, self.r1, self.s2, self.r2, self.s3, self.r3, self.s4, self.r4) = sems
        lat, lon, self.core, depth, plane = place()
        self.sibling = (lat, lon + 1 - 2 * self.core)
        x, y = lax.rem(lat, 4), lax.div(lat, 4) * 2 + lax.div(lon, 16)
        planes, depths = [], []
        for kx, ky in sorted(((a, b) for a in range(4) for b in range(4) if a or b),
                             key=lambda k: -min(k[0], 4 - k[0]) - min(k[1], 4 - k[1])):
            to_x, to_y = lax.rem(x + kx, 4), lax.rem(y + ky, 4)
            to_lat, to_part = lax.div(to_y, 2) * 4 + to_x, lax.rem(to_y, 2)
            planes.append((to_lat * 2 + to_part, (to_lat, to_part * 16 + lax.rem(lon, 16))))
        for k in sorted(range(1, DEPTH), key=lambda k: -min(k, DEPTH - k)):
            to = lax.rem(depth + k, DEPTH)
            depths.append((to, (lat, lax.div(lon, 16) * 16 + to * 2 + self.core)))
        groups = ((plane, planes), (depth, depths))
        (self.me1, self.peers1), (self.me2, self.peers2) = groups if plane_first else groups[::-1]
        self.across = 4 if plane_first else 2

    def piece(self, index, base=0):
        width = HID // self.across
        row = pl.multiple_of(base + lax.div(index, self.across) * 16, 16)
        lane = pl.multiple_of(lax.rem(index, self.across) * width, width)
        return (slice(None), pl.ds(row, 16), pl.ds(lane, width))

    def copy0(self):
        return pltpu.make_async_remote_copy(
            src_ref=self.send0, dst_ref=self.recv0, send_sem=self.s0, recv_sem=self.r0,
            device_id=self.sibling, device_id_type=MESH)

    def copies1(self):
        return [pltpu.make_async_remote_copy(
            src_ref=self.send1.at[self.piece(to)], dst_ref=self.recv1.at[n],
            send_sem=self.s1, recv_sem=self.r1,
            device_id=device, device_id_type=MESH) for n, (to, device) in enumerate(self.peers1)]

    def copies2(self):
        mine = self.recv2.at[self.me2]
        return [pltpu.make_async_remote_copy(
            src_ref=mine, dst_ref=mine, send_sem=self.s2, recv_sem=self.r2,
            device_id=device, device_id_type=MESH) for _, device in self.peers2]

    def copies3(self):
        mine = self.full.at[self.piece(self.me1, 64 * self.core)]
        return [pltpu.make_async_remote_copy(
            src_ref=mine, dst_ref=mine, send_sem=self.s3, recv_sem=self.r3,
            device_id=device, device_id_type=MESH) for _, device in self.peers1]

    def all_of(self, ref, send_sem, recv_sem):
        return pltpu.make_async_remote_copy(
            src_ref=ref, dst_ref=ref, send_sem=send_sem, recv_sem=recv_sem,
            device_id=self.sibling, device_id_type=MESH)

    def copy4(self):
        mine = self.full.at[:, pl.ds(pl.multiple_of(64 * self.core, 64), 64), :]
        return pltpu.make_async_remote_copy(
            src_ref=mine, dst_ref=mine, send_sem=self.s4, recv_sem=self.r4,
            device_id=self.sibling, device_id_type=MESH)

    def step0(self):
        other = pl.multiple_of(64 * (1 - self.core), 64)
        self.send0[...] = self.part[:, pl.ds(other, 64), :].astype(BF)
        self.copy0().start()

    def step1(self):
        self.copy0().wait()
        mine = pl.multiple_of(64 * self.core, 64)
        self.half[...] = self.part[:, pl.ds(mine, 64), :] + self.recv0[...].astype(F32)
        self.send1[...] = self.half[...].astype(BF)
        for copy in self.copies1():
            copy.start()

    def step2(self):
        self.all_of(self.recv1, self.s1, self.r1).wait()
        total = self.half[self.piece(self.me1)]
        for n in range(len(self.peers1)):
            total = total + self.recv1[n].astype(F32)
        self.recv2[self.me2] = total.astype(BF)
        for copy in self.copies2():
            copy.start()

    def step3(self):
        self.all_of(self.recv2.at[pl.ds(0, len(self.peers2))], self.s2, self.r2).wait()
        total = self.recv2[0].astype(F32)
        for n in range(1, len(self.peers2) + 1):
            total = total + self.recv2[n].astype(F32)
        self.full[self.piece(self.me1, 64 * self.core)] = total.astype(BF)
        for copy in self.copies3():
            copy.start()

    def step4(self):
        self.all_of(self.recv1, self.s3, self.r3).wait()
        self.copy4().start()

    def finish(self):
        self.copy4().wait()


def kernel(scale, rounds, state_hbm, heat_hbm, scot_hbm, clon_hbm, clat_hbm, w1_hbm, w2_hbm, w3_hbm,
           out_hbm, first_hbm, second_hbm, third_hbm,
           nat_a, nat_b, state, heat, scot, clon, clat, w1, w2, w3, w1t, w2t, w3t,
           normed_s, inv_s, inputs_s, act1_s, slope1_s, back2_s, act2_s, back1_s, part,
           cot_a, cot_b, high_s, low_s, sides_s, east_f, west_f, north_f, south_f, ends_f,
           shift_m, ends_m, pack_m, out_nat, first, second, third,
           rim_send, rim_recv, row_send, row_recv,
           load_sem, store_sem, second_sem, rim_ss, rim_rs, row_ss, row_rs,
           *rest):
    lat, lon, core, depth, plane = place()
    lats, lons = lax.axis_size("lat"), lax.axis_size("lon")
    west_id = (lat, lax.rem(lon + lons - 1, lons))
    east_id = (lat, lax.rem(lon + 1, lons))
    up, down = lat < lats - 1, lat > 0
    reds = []
    for n, (lo, count, plane_first) in enumerate(rounds):
        own = rest[17 * n:17 * (n + 1)]
        reds.append(Reduction(part.at[pl.ds(lo, count)], plane_first, own[:7], own[7:]))
    early = reds[:-1]

    barrier = pltpu.get_barrier_semaphore()

    def greet(device):
        pl.semaphore_signal(barrier, inc=1, device_id=device, device_id_type=MESH)

    for _, device in reds[0].peers1 + reds[0].peers2:
        greet(device)
    greet(reds[0].sibling)
    greet(west_id)
    greet(east_id)

    loads = [pltpu.make_async_copy(src, dst, load_sem.at[i]) for i, (src, dst) in
             enumerate(((state_hbm, state), (w1_hbm, w1), (w2_hbm, w2), (w3_hbm, w3), (heat_hbm, heat),
                        (clon_hbm, clon), (clat_hbm, clat), (scot_hbm, scot)))]
    for load in loads:
        load.start()

    down_i = lax.broadcasted_iota(jnp.int32, (LEV, LON), 0)
    lane = lax.broadcasted_iota(jnp.int32, (LEV, LON), 1)
    for half in range(2):
        shift_m[half * LON:(half + 1) * LON, :LON] = (down_i == lane + 1).astype(BF)
        shift_m[half * LON:(half + 1) * LON, LON:] = (down_i + 1 == lane).astype(BF)
    for row in range(ROWS):
        cols = slice(row * LON, (row + 1) * LON)
        ends_m[:LON, cols] = jnp.where((down_i == 2 * row) & (lane == 0), 1.0, 0.0).astype(BF)
        ends_m[LON:, cols] = jnp.where(
            (down_i == 2 * row + 1) & (lane == LON - 1), 1.0, 0.0).astype(BF)
        pack_m[cols, :] = jnp.where(
            ((down_i == LON - 1) & (lane == 2 * row)) | ((down_i == 0) & (lane == 2 * row + 1)),
            1.0, 0.0).astype(BF)
    cot_a[0] = jnp.zeros((LEV, LON), F32)
    cot_b[0] = jnp.zeros((LEV, LON), F32)
    cot_a[ROWS + 1] = jnp.zeros((LEV, LON), F32)
    cot_b[ROWS + 1] = jnp.zeros((LEV, LON), F32)

    @pl.when(jnp.logical_not(down))
    def _():
        for slot in range(SUBSTEPS + 1):
            row_recv[slot, 0] = jnp.zeros((LEV, LON), BF)

    @pl.when(jnp.logical_not(up))
    def _():
        for slot in range(SUBSTEPS):
            row_recv[slot, 1] = jnp.zeros((LEV, LON), BF)

    for load in loads[:5]:
        load.wait()
    nat_a[...] = state[...].astype(F32)
    nat_b[...] = heat[...].astype(F32)
    w1t[...] = w1[...].T
    w2t[...] = w2[...].T
    w3t[...] = w3[...].T

    def rows_of(ref, first):
        return jnp.concatenate(
            [ref[pl.ds(first + i, LEV, stride=ROWS), :] for i in range(CHUNK_ROWS)], axis=1)

    blocks = [slice(128 * m, 128 * (m + 1)) for m in range(4)]

    def add_blocks(index, terms, new):
        for m in blocks:
            part[index, :, m] = terms[m, :] if new else part[index, :, m] + terms[m, :]

    def forward(chunk):
        cols = slice(chunk * CHUNK, (chunk + 1) * CHUNK)
        values = rows_of(nat_a, chunk * CHUNK_ROWS)
        inverse = lax.rsqrt(jnp.mean(values * values, axis=0, keepdims=True) + EPSILON)
        normed = values * inverse
        inputs = normed.astype(BF)
        normed_s[:, cols] = normed
        inv_s[:, cols] = inverse
        inputs_s[:, cols] = inputs
        cot = rows_of(nat_b, chunk * CHUNK_ROWS).astype(BF)
        act, slope = silu_and_slope(dot(w1[...], inputs))
        act1_s[:, cols] = act.astype(BF)
        slope1_s[:, cols] = slope
        act, slope = silu_and_slope(dot(w2[...], act1_s[:, cols]))
        act2_s[chunk % 2] = act.astype(BF)
        back2_s[:, cols] = (dot(w3t[...], cot) * slope).astype(BF)
        add_blocks(4, dot_last(act2_s[chunk % 2], cot), chunk == 0)
        terms = dot_last(back2_s[:, cols], act1_s[:, cols]).reshape(4, 128, HID)
        part[:4] = terms if chunk == 0 else part[:4] + terms

    for chunk in range(CHUNKS):
        forward(chunk)
    pl.semaphore_wait(barrier, (PLANE - 1) + (DEPTH - 1) + 3)
    for red in early:
        red.step0()

    def rim_copy(slot, way):
        return pltpu.make_async_remote_copy(
            src_ref=rim_send.at[slot], dst_ref=rim_recv.at[slot, way],
            send_sem=rim_ss.at[slot, way], recv_sem=rim_rs.at[slot, way],
            device_id=(east_id, west_id)[way], device_id_type=MESH)

    def row_copy(slot, way):
        return pltpu.make_async_remote_copy(
            src_ref=row_send.at[slot, way], dst_ref=row_recv.at[slot, way],
            send_sem=row_ss.at[slot, way], recv_sem=row_rs.at[slot, way],
            device_id=(jnp.clip(lat + (1, -1)[way], 0, lats - 1), lon), device_id_type=MESH)

    def send_rows(slot, ways):
        for way in ways:
            pl.when((up, down)[way])(lambda: row_copy(slot, way).start())

    def wait_rows(slot, ways):
        for way in ways:
            pl.when((up, down)[way])(lambda: row_copy(slot, way).wait_send())
            pl.when((down, up)[way])(lambda: row_copy(slot, way).wait_recv())

    def backward(chunk):
        cols = slice(chunk * CHUNK, (chunk + 1) * CHUNK)
        back1_s[:, cols] = (dot(w2t[...], back2_s[:, cols]) * slope1_s[:, cols]).astype(BF)
        add_blocks(5, dot_last(back1_s[:, cols], inputs_s[:, cols]), chunk == 0)

    def input_part(chunk):
        cols = slice(chunk * CHUNK, (chunk + 1) * CHUNK)
        input_cot = dot(w1t[...], back1_s[:, cols])
        normed = normed_s[:, cols]
        state_part = inv_s[:, cols] * (
            input_cot - normed * jnp.mean(input_cot * normed, axis=0, keepdims=True))
        for i in range(CHUNK_ROWS):
            row = chunk * CHUNK_ROWS + i
            keep(row, state_part[:, i * LON:(i + 1) * LON] + scot[pl.ds(row, LEV, stride=ROWS), :],
                 cot_a)

    def keep(row, new, cells):
        cells[row + 1] = new
        high = new.astype(BF)
        high_s[row] = high
        low_s[row] = (new - high.astype(F32)).astype(BF)

    def packed():
        return sum(dot(jnp.concatenate([high_s[row], high_s[row + 1]], axis=1),
                       pack_m[row * LON:(row + 2) * LON, :]) for row in range(0, ROWS, 2)).astype(BF)

    for chunk in range(CHUNKS // 2):
        backward(chunk)
    for red in early:
        red.step1()
    for chunk in range(CHUNKS // 2, CHUNKS):
        backward(chunk)
    reds[-1].step0()
    loads[7].wait()
    for chunk in range(CHUNKS):
        input_part(chunk)
    reds[-1].step1()

    def send_halo(slot):
        row_send[slot, 0] = high_s[ROWS - 1]
        row_send[slot, 1] = high_s[0]
        send_rows(slot, (0, 1))
        rim_send[slot] = packed()
        rim_copy(slot, 0).start()
        rim_copy(slot, 1).start()

    loads[5].wait()
    loads[6].wait()
    nat_a[...] = clon[...].astype(F32)
    nat_b[...] = clat[...].astype(F32)
    row_send[SUBSTEPS, 0] = nat_b[pl.ds(ROWS - 1, LEV, stride=ROWS), :].astype(BF)
    send_rows(SUBSTEPS, (0,))
    faces_pairs = [jnp.concatenate(
        [nat_a[pl.ds(row + i, LEV, stride=ROWS), :].astype(BF) for i in range(2)], axis=1)
        for row in range(0, ROWS, 2)]
    rim_send[SUBSTEPS] = sum(dot(pair, pack_m[2 * i * LON:2 * (i + 1) * LON, :])
                             for i, pair in enumerate(faces_pairs)).astype(BF)
    rim_copy(SUBSTEPS, 0).start()
    send_halo(0)

    def sides():
        sides_s[...] = dot(jnp.concatenate(
            [high_s[...].reshape(COLS, LON), low_s[...].reshape(COLS, LON)], axis=1), shift_m[...])

    sides()

    def split_lat(row):
        ahead = nat_b[pl.ds(row, LEV, stride=ROWS), :]
        north_f[row] = jnp.maximum(ahead, 0.0)
        south_f[row + 1] = jnp.minimum(ahead, 0.0)

    loop(0, ROWS, split_lat)
    rim_copy(SUBSTEPS, 0).wait()
    wait_rows(SUBSTEPS, (0,))
    south_f[0] = jnp.minimum(row_recv[SUBSTEPS, 0].astype(F32), 0.0)
    west_rim = rim_recv[SUBSTEPS, 0]
    for row in range(ROWS):
        faces = nat_a[pl.ds(row, LEV, stride=ROWS), :]
        west = dot(jnp.concatenate([faces.astype(BF), west_rim], axis=1), jnp.concatenate(
            [shift_m[:LON, LON:], ends_m[:LON, row * LON:(row + 1) * LON]], axis=0))
        west = jnp.minimum(west, 0.0)
        faces = jnp.maximum(faces, 0.0)
        east_f[row] = faces
        west_f[row] = west
        ends_f[row] = jnp.where(lane == LON - 1, faces, jnp.where(lane == 0, -west, 0.0))

    def inner(cells, new_cells):
        def one_row(row):
            centre = cells[row + 1]
            here = pl.ds(pl.multiple_of(row * LEV, LEV), LEV)
            new_cells[row + 1] = (
                centre + east_f[row] * (sides_s[here, :LON] - centre)
                + west_f[row] * (centre - sides_s[here, LON:])
                + north_f[row] * (cells[row + 2] - centre)
                + south_f[row] * (centre - cells[row]))

        loop(0, ROWS, one_row)

    def outer(slot, new_cells, store):
        rim_copy(slot, 0).wait()
        rim_copy(slot, 1).wait()
        wait_rows(slot, (0, 1))
        rims = jnp.concatenate([rim_recv[slot, 0], rim_recv[slot, 1]], axis=1)
        for row in range(0, ROWS, 2):
            ends = dot(rims, ends_m[:, row * LON:(row + 2) * LON])
            for i in range(2):
                new = new_cells[row + i + 1] + ends_f[row + i] * ends[:, i * LON:(i + 1) * LON]
                if row + i == 0:
                    new = new - south_f[0] * row_recv[slot, 0].astype(F32)
                if row + i == ROWS - 1:
                    new = new + north_f[ROWS - 1] * row_recv[slot, 1].astype(F32)
                store(row + i, new, new_cells)

    def into_natural(row, new, cells):
        out_nat[pl.ds(row, LEV, stride=ROWS), :] = new

    stores = [pltpu.make_async_copy(src, dst, store_sem.at[i]) for i, (src, dst) in enumerate(
        ((out_nat, out_hbm), (first, first_hbm), (third, third_hbm)))]

    third_red, second_red, first_red = reds
    def put_second(other):
        base = pl.multiple_of(64 * (1 - core if other else core), 64)
        for i in range(4):
            rows = pl.ds(pl.multiple_of(128 * i + base, 64), 64)
            second[rows, :] = second_red.full[i, pl.ds(base, 64), :].astype(F32) * scale
            store = pltpu.make_async_copy(second.at[rows], second_hbm.at[rows], second_sem.at[other, i])
            store.start()
            stores.append(store)

    inner(cot_a, cot_b)
    third_red.step2()
    second_red.step2()
    outer(0, cot_b, keep)
    send_halo(1)
    first_red.step2()
    sides()
    inner(cot_b, cot_a)
    third_red.step3()
    outer(1, cot_a, keep)
    send_halo(2)
    sides()
    inner(cot_a, cot_b)
    second_red.step3()
    first_red.step3()
    third_red.step4()
    outer(2, cot_b, into_natural)
    stores[0].start()
    first_red.step4()
    second_red.step4()
    put_second(0)
    third_red.finish()

    def total(index):
        for (lo, count, _), red in zip(rounds, reds):
            if lo <= index < lo + count:
                return red.full[index - lo].astype(F32) * scale

    sum_third = total(4)
    for m in blocks:
        third[:, m] = sum_third[:, m].T
    stores[2].start()
    first_red.finish()
    sum_first = total(5)
    for m in blocks:
        first[m, :] = sum_first[:, m]
    stores[1].start()
    second_red.finish()
    put_second(1)
    for store in stores:
        store.wait()


def reduction_scratch(nb, plane_first):
    n1, n2 = (PLANE, DEPTH) if plane_first else (DEPTH, PLANE)
    width = HID * 4 // n1
    half, piece = (nb, 64, HID), (nb, 16, width)
    bufs = [
        pltpu.VMEM(half, BF), pltpu.VMEM(half, BF), pltpu.VMEM(half, F32), pltpu.VMEM(half, BF),
        pltpu.VMEM((n1 - 1,) + piece, BF), pltpu.VMEM((n2,) + piece, BF), pltpu.VMEM((nb, 128, HID), BF),
    ]
    dma = pltpu.SemaphoreType.DMA
    return bufs + [dma] * 10


def finish_kernel(*refs):
    ins, outs, held, load_sem, store_sem = refs[:4], refs[4:8], refs[8:12], refs[12], refs[13]
    moves = []
    for src, dst, buf in zip(ins, outs, held):
        size = min(src.shape[0], FINISH_ROWS * 128 // src.shape[1])
        for first in range(0, src.shape[0], size):
            rows = pl.ds(first, size)
            n = len(moves)
            moves.append((
                pltpu.make_async_copy(src.at[rows], buf.at[rows], load_sem.at[n]),
                pltpu.make_async_copy(buf.at[rows], dst.at[rows], store_sem.at[n])))
    for load, _ in moves:
        load.start()
    for load, store in moves:
        load.wait()
        store.start()
    for _, store in moves:
        store.wait()


def local(state, heat_cot, state_cot, courant_lon, courant_lat, w_first, w_second, w_third):
    levels, lat_rows, lon_cols = state.shape
    scale = 1.0 / math.sqrt(lat_rows * lon_cols * lax.axis_size("lat") * lax.axis_size("lon"))
    flat = (levels * lat_rows, lon_cols)
    hbm = pl.BlockSpec(memory_space=pl.ANY)
    dma = pltpu.SemaphoreType.DMA
    tile = (LEV, LON)
    bfs = lambda *shapes: [pltpu.VMEM(shape, BF) for shape in shapes]
    f32s = lambda *shapes: [pltpu.VMEM(shape, F32) for shape in shapes]
    grid = (ROWS,) + tile
    halo = (SUBSTEPS + 1, 2)
    scratch = [
        *f32s(flat, flat), *bfs(flat, flat), *f32s(flat), *bfs(flat, flat),
        *bfs((HID, LEV), (HID, HID), (LEV, HID), (LEV, HID), (HID, HID), (HID, LEV)),
        *f32s((LEV, COLS), (1, COLS)), *bfs((LEV, COLS), (HID, COLS)), *f32s((HID, COLS)),
        *bfs((HID, COLS), (2, HID, CHUNK), (HID, COLS)), *f32s((6, 128, 512)),
        *f32s((ROWS + 2,) + tile, (ROWS + 2,) + tile), *bfs(grid, grid), *f32s((COLS, 2 * LON)),
        *f32s(grid, grid, grid, (ROWS + 1,) + tile, grid),
        *bfs((2 * LON, 2 * LON), (2 * LON, COLS), (COLS, LON)),
        *f32s(flat, (HID, LEV), (HID, HID), (LEV, HID)),
        *bfs((SUBSTEPS + 1,) + tile, halo + tile, halo + tile, halo + tile),
        dma((8,)), dma((3,)), dma((2, 4)), dma(halo), dma(halo), dma(halo), dma(halo),
    ]
    for _, count, plane_first in ROUNDS:
        scratch += reduction_scratch(count, plane_first)
    shapes = (flat, (HID, LEV), (HID, HID), (LEV, HID))
    results = tuple(jax.ShapeDtypeStruct(shape, F32) for shape in shapes)
    out = pl.pallas_call(
        functools.partial(kernel, scale, ROUNDS),
        out_shape=results,
        in_specs=[hbm] * 8,
        out_specs=(hbm,) * 4,
        scratch_shapes=scratch,
        compiler_params=pltpu.CompilerParams(
            collective_id=0, has_side_effects=True, vmem_limit_bytes=60 << 20),
    )(state.reshape(flat), heat_cot.reshape(flat), state_cot.reshape(flat),
      courant_lon.reshape(flat), courant_lat.reshape(flat), w_first, w_second, w_third)
    grid, first, second, third = pl.pallas_call(
        finish_kernel, out_shape=results, in_specs=[hbm] * 4, out_specs=(hbm,) * 4,
        scratch_shapes=[*f32s(*shapes), dma((16,)), dma((16,))],
        compiler_params=pltpu.CompilerParams(vmem_limit_bytes=60 << 20),
    )(*out)
    return grid.reshape(state.shape), first, second, third


def solution(mesh):
    split = P(None, "lat", "lon")
    return jax.shard_map(
        local, mesh=mesh, in_specs=(split,) * 5 + (P(),) * 3,
        out_specs=(split, P(), P(), P()), check_vma=False)
```

```python
import functools
import math

import jax
import jax.numpy as jnp
from jax import lax
from jax.experimental import pallas as pl
from jax.experimental.pallas import tpu as pltpu
from jax.sharding import PartitionSpec as P

EPSILON = 1e-05
SUBSTEPS = 3
MESH = pl.DeviceIdType.MESH
BF = jnp.bfloat16
F32 = jnp.float32
LEV = 128
HID = 512
ROWS = 16
LON = 128
COLS = ROWS * LON
CHUNK_ROWS = 4
CHUNK = CHUNK_ROWS * LON
CHUNKS = ROWS // CHUNK_ROWS
PLANE = 16
DEPTH = 8
ROUNDS = ((4, 1, False), (0, 4, True), (5, 1, False))
FINISH_ROWS = 512


def dot(a, b):
    return jnp.dot(a, b, preferred_element_type=F32)


def dot_last(a, b):
    return lax.dot_general(a, b, (((1,), (1,)), ((), ())), preferred_element_type=F32)


def silu_and_slope(pre):
    sigma = 0.5 * jnp.tanh(0.5 * pre) + 0.5
    act = pre * sigma
    return act, sigma + act * (1.0 - sigma)


def place():
    lat, lon = lax.axis_index("lat"), lax.axis_index("lon")
    core = lax.rem(lon, 2)
    depth = lax.rem(lax.div(lon, 2), DEPTH)
    plane = lat * 2 + lax.div(lon, 16)
    return lat, lon, core, depth, plane


def loop(lo, hi, body):
    lax.fori_loop(lo, hi, lambda k, carry: (body(k), carry)[1], 0)


class Reduction:
    def __init__(self, part, plane_first, bufs, sems):
        self.part = part
        self.send0, self.recv0, self.half, self.send1, self.recv1, self.recv2, self.full = bufs
        (self.s0, self.r0, self.s1, self.r1, self.s2, self.r2, self.s3, self.r3, self.s4, self.r4) = sems
        lat, lon, self.core, depth, plane = place()
        self.sibling = (lat, lon + 1 - 2 * self.core)
        x, y = lax.rem(lat, 4), lax.div(lat, 4) * 2 + lax.div(lon, 16)
        planes, depths = [], []
        for kx, ky in sorted(((a, b) for a in range(4) for b in range(4) if a or b),
                             key=lambda k: -min(k[0], 4 - k[0]) - min(k[1], 4 - k[1])):
            to_x, to_y = lax.rem(x + kx, 4), lax.rem(y + ky, 4)
            to_lat, to_part = lax.div(to_y, 2) * 4 + to_x, lax.rem(to_y, 2)
            planes.append((to_lat * 2 + to_part, (to_lat, to_part * 16 + lax.rem(lon, 16))))
        for k in sorted(range(1, DEPTH), key=lambda k: -min(k, DEPTH - k)):
            to = lax.rem(depth + k, DEPTH)
            depths.append((to, (lat, lax.div(lon, 16) * 16 + to * 2 + self.core)))
        groups = ((plane, planes), (depth, depths))
        (self.me1, self.peers1), (self.me2, self.peers2) = groups if plane_first else groups[::-1]
        self.across = 4 if plane_first else 2

    def piece(self, index, base=0):
        width = HID // self.across
        row = pl.multiple_of(base + lax.div(index, self.across) * 16, 16)
        lane = pl.multiple_of(lax.rem(index, self.across) * width, width)
        return (slice(None), pl.ds(row, 16), pl.ds(lane, width))

    def copy0(self):
        return pltpu.make_async_remote_copy(
            src_ref=self.send0, dst_ref=self.recv0, send_sem=self.s0, recv_sem=self.r0,
            device_id=self.sibling, device_id_type=MESH)

    def copies1(self):
        return [pltpu.make_async_remote_copy(
            src_ref=self.send1.at[self.piece(to)], dst_ref=self.recv1.at[n],
            send_sem=self.s1, recv_sem=self.r1,
            device_id=device, device_id_type=MESH) for n, (to, device) in enumerate(self.peers1)]

    def copies2(self):
        mine = self.recv2.at[self.me2]
        return [pltpu.make_async_remote_copy(
            src_ref=mine, dst_ref=mine, send_sem=self.s2, recv_sem=self.r2,
            device_id=device, device_id_type=MESH) for _, device in self.peers2]

    def copies3(self):
        mine = self.full.at[self.piece(self.me1, 64 * self.core)]
        return [pltpu.make_async_remote_copy(
            src_ref=mine, dst_ref=mine, send_sem=self.s3, recv_sem=self.r3,
            device_id=device, device_id_type=MESH) for _, device in self.peers1]

    def all_of(self, ref, send_sem, recv_sem):
        return pltpu.make_async_remote_copy(
            src_ref=ref, dst_ref=ref, send_sem=send_sem, recv_sem=recv_sem,
            device_id=self.sibling, device_id_type=MESH)

    def copy4(self):
        mine = self.full.at[:, pl.ds(pl.multiple_of(64 * self.core, 64), 64), :]
        return pltpu.make_async_remote_copy(
            src_ref=mine, dst_ref=mine, send_sem=self.s4, recv_sem=self.r4,
            device_id=self.sibling, device_id_type=MESH)

    def step0(self):
        other = pl.multiple_of(64 * (1 - self.core), 64)
        self.send0[...] = self.part[:, pl.ds(other, 64), :].astype(BF)
        self.copy0().start()

    def step1(self):
        self.copy0().wait()
        mine = pl.multiple_of(64 * self.core, 64)
        self.half[...] = self.part[:, pl.ds(mine, 64), :] + self.recv0[...].astype(F32)
        self.send1[...] = self.half[...].astype(BF)
        for copy in self.copies1():
            copy.start()

    def step2(self):
        self.all_of(self.recv1, self.s1, self.r1).wait()
        total = self.half[self.piece(self.me1)]
        for n in range(len(self.peers1)):
            total = total + self.recv1[n].astype(F32)
        self.recv2[self.me2] = total.astype(BF)
        for copy in self.copies2():
            copy.start()

    def step3(self):
        self.all_of(self.recv2.at[pl.ds(0, len(self.peers2))], self.s2, self.r2).wait()
        total = self.recv2[0].astype(F32)
        for n in range(1, len(self.peers2) + 1):
            total = total + self.recv2[n].astype(F32)
        self.full[self.piece(self.me1, 64 * self.core)] = total.astype(BF)
        for copy in self.copies3():
            copy.start()

    def step4(self):
        self.all_of(self.recv1, self.s3, self.r3).wait()
        self.copy4().start()

    def finish(self):
        self.copy4().wait()


def kernel(scale, rounds, state_hbm, heat_hbm, scot_hbm, clon_hbm, clat_hbm, w1_hbm, w2_hbm, w3_hbm,
           out_hbm, first_hbm, second_hbm, third_hbm,
           nat_a, nat_b, state, heat, scot, clon, clat, w1, w2, w3, w1t, w2t, w3t,
           normed_s, inv_s, inputs_s, act1_s, slope1_s, back2_s, act2_s, part,
           cot_a, cot_b, high_s, low_s, sides_s, east_f, west_f, north_f, south_f, ends_f,
           shift_m, ends_m, pack_m, out_nat, first, second, third,
           rim_send, rim_recv, row_send, row_recv,
           load_sem, store_sem, rim_ss, rim_rs, row_ss, row_rs,
           *rest):
    lat, lon, core, depth, plane = place()
    lats, lons = lax.axis_size("lat"), lax.axis_size("lon")
    west_id = (lat, lax.rem(lon + lons - 1, lons))
    east_id = (lat, lax.rem(lon + 1, lons))
    up, down = lat < lats - 1, lat > 0
    reds = []
    for n, (lo, count, plane_first) in enumerate(rounds):
        own = rest[17 * n:17 * (n + 1)]
        reds.append(Reduction(part.at[pl.ds(lo, count)], plane_first, own[:7], own[7:]))
    early = reds[:-1]

    barrier = pltpu.get_barrier_semaphore()

    def greet(device):
        pl.semaphore_signal(barrier, inc=1, device_id=device, device_id_type=MESH)

    for _, device in reds[0].peers1 + reds[0].peers2:
        greet(device)
    greet(reds[0].sibling)
    greet(west_id)
    greet(east_id)

    loads = [pltpu.make_async_copy(src, dst, load_sem.at[i]) for i, (src, dst) in
             enumerate(((state_hbm, state), (w1_hbm, w1), (w2_hbm, w2), (w3_hbm, w3), (heat_hbm, heat),
                        (clon_hbm, clon), (clat_hbm, clat), (scot_hbm, scot)))]
    for load in loads:
        load.start()

    down_i = lax.broadcasted_iota(jnp.int32, (LEV, LON), 0)
    lane = lax.broadcasted_iota(jnp.int32, (LEV, LON), 1)
    for half in range(2):
        shift_m[half * LON:(half + 1) * LON, :LON] = (down_i == lane + 1).astype(BF)
        shift_m[half * LON:(half + 1) * LON, LON:] = (down_i + 1 == lane).astype(BF)
    for row in range(ROWS):
        cols = slice(row * LON, (row + 1) * LON)
        ends_m[:LON, cols] = jnp.where((down_i == 2 * row) & (lane == 0), 1.0, 0.0).astype(BF)
        ends_m[LON:, cols] = jnp.where(
            (down_i == 2 * row + 1) & (lane == LON - 1), 1.0, 0.0).astype(BF)
        pack_m[cols, :] = jnp.where(
            ((down_i == LON - 1) & (lane == 2 * row)) | ((down_i == 0) & (lane == 2 * row + 1)),
            1.0, 0.0).astype(BF)
    cot_a[0] = jnp.zeros((LEV, LON), F32)
    cot_b[0] = jnp.zeros((LEV, LON), F32)
    cot_a[ROWS + 1] = jnp.zeros((LEV, LON), F32)
    cot_b[ROWS + 1] = jnp.zeros((LEV, LON), F32)

    @pl.when(jnp.logical_not(down))
    def _():
        for slot in range(SUBSTEPS + 1):
            row_recv[slot, 0] = jnp.zeros((LEV, LON), BF)

    @pl.when(jnp.logical_not(up))
    def _():
        for slot in range(SUBSTEPS):
            row_recv[slot, 1] = jnp.zeros((LEV, LON), BF)

    for load in loads[:5]:
        load.wait()
    nat_a[...] = state[...].astype(F32)
    nat_b[...] = heat[...].astype(F32)
    w1t[...] = w1[...].T
    w2t[...] = w2[...].T
    w3t[...] = w3[...].T

    def rows_of(ref, first):
        return jnp.concatenate(
            [ref[pl.ds(first + i, LEV, stride=ROWS), :] for i in range(CHUNK_ROWS)], axis=1)

    blocks = [slice(128 * m, 128 * (m + 1)) for m in range(4)]

    def add_blocks(index, terms, new):
        for m in blocks:
            part[index, :, m] = terms[m, :] if new else part[index, :, m] + terms[m, :]

    def forward(chunk):
        cols = slice(chunk * CHUNK, (chunk + 1) * CHUNK)
        values = rows_of(nat_a, chunk * CHUNK_ROWS)
        inverse = lax.rsqrt(jnp.mean(values * values, axis=0, keepdims=True) + EPSILON)
        normed = values * inverse
        inputs = normed.astype(BF)
        normed_s[:, cols] = normed
        inv_s[:, cols] = inverse
        inputs_s[:, cols] = inputs
        cot = rows_of(nat_b, chunk * CHUNK_ROWS).astype(BF)
        act, slope = silu_and_slope(dot(w1[...], inputs))
        act1_s[:, cols] = act.astype(BF)
        slope1_s[:, cols] = slope
        act, slope = silu_and_slope(dot(w2[...], act1_s[:, cols]))
        act2_s[chunk % 2] = act.astype(BF)
        back2_s[:, cols] = (dot(w3t[...], cot) * slope).astype(BF)
        add_blocks(4, dot_last(act2_s[chunk % 2], cot), chunk == 0)
        terms = dot_last(back2_s[:, cols], act1_s[:, cols]).reshape(4, 128, HID)
        part[:4] = terms if chunk == 0 else part[:4] + terms

    for chunk in range(CHUNKS):
        forward(chunk)
    pl.semaphore_wait(barrier, (PLANE - 1) + (DEPTH - 1) + 3)
    for red in early:
        red.step0()

    def rim_copy(slot, way):
        return pltpu.make_async_remote_copy(
            src_ref=rim_send.at[slot], dst_ref=rim_recv.at[slot, way],
            send_sem=rim_ss.at[slot, way], recv_sem=rim_rs.at[slot, way],
            device_id=(east_id, west_id)[way], device_id_type=MESH)

    def row_copy(slot, way):
        return pltpu.make_async_remote_copy(
            src_ref=row_send.at[slot, way], dst_ref=row_recv.at[slot, way],
            send_sem=row_ss.at[slot, way], recv_sem=row_rs.at[slot, way],
            device_id=(jnp.clip(lat + (1, -1)[way], 0, lats - 1), lon), device_id_type=MESH)

    def send_rows(slot, ways):
        for way in ways:
            pl.when((up, down)[way])(lambda: row_copy(slot, way).start())

    def wait_rows(slot, ways):
        for way in ways:
            pl.when((up, down)[way])(lambda: row_copy(slot, way).wait_send())
            pl.when((down, up)[way])(lambda: row_copy(slot, way).wait_recv())

    def backward(chunk):
        cols = slice(chunk * CHUNK, (chunk + 1) * CHUNK)
        back = (dot(w2t[...], back2_s[:, cols]) * slope1_s[:, cols]).astype(BF)
        act2_s[chunk % 2] = back
        add_blocks(5, dot_last(back, inputs_s[:, cols]), chunk == 0)
        input_cot = dot(w1t[...], act2_s[chunk % 2])
        normed = normed_s[:, cols]
        state_part = inv_s[:, cols] * (
            input_cot - normed * jnp.mean(input_cot * normed, axis=0, keepdims=True))
        for i in range(CHUNK_ROWS):
            row = chunk * CHUNK_ROWS + i
            keep(row, state_part[:, i * LON:(i + 1) * LON] + scot[pl.ds(row, LEV, stride=ROWS), :],
                 cot_a)

    def keep(row, new, cells):
        cells[row + 1] = new
        high = new.astype(BF)
        high_s[row] = high
        low_s[row] = (new - high.astype(F32)).astype(BF)

    def packed():
        return sum(dot(jnp.concatenate([high_s[row], high_s[row + 1]], axis=1),
                       pack_m[row * LON:(row + 2) * LON, :]) for row in range(0, ROWS, 2)).astype(BF)

    loads[5].wait()
    loads[6].wait()
    nat_a[...] = clon[...].astype(F32)
    nat_b[...] = clat[...].astype(F32)
    row_send[SUBSTEPS, 0] = nat_b[pl.ds(ROWS - 1, LEV, stride=ROWS), :].astype(BF)
    send_rows(SUBSTEPS, (0,))
    faces_pairs = [jnp.concatenate(
        [nat_a[pl.ds(row + i, LEV, stride=ROWS), :].astype(BF) for i in range(2)], axis=1)
        for row in range(0, ROWS, 2)]
    rim_send[SUBSTEPS] = sum(dot(pair, pack_m[2 * i * LON:2 * (i + 1) * LON, :])
                             for i, pair in enumerate(faces_pairs)).astype(BF)
    rim_copy(SUBSTEPS, 0).start()
    loads[7].wait()
    backward(0)
    for red in early:
        red.step1()
    for chunk in range(1, CHUNKS):
        backward(chunk)
    reds[-1].step0()

    def send_halo(slot):
        row_send[slot, 0] = high_s[ROWS - 1]
        row_send[slot, 1] = high_s[0]
        send_rows(slot, (0, 1))
        rim_send[slot] = packed()
        rim_copy(slot, 0).start()
        rim_copy(slot, 1).start()

    send_halo(0)

    def sides():
        sides_s[...] = dot(jnp.concatenate(
            [high_s[...].reshape(COLS, LON), low_s[...].reshape(COLS, LON)], axis=1), shift_m[...])

    sides()

    def split_lat(row):
        ahead = nat_b[pl.ds(row, LEV, stride=ROWS), :]
        north_f[row] = jnp.maximum(ahead, 0.0)
        south_f[row + 1] = jnp.minimum(ahead, 0.0)

    loop(0, ROWS, split_lat)
    reds[-1].step1()
    rim_copy(SUBSTEPS, 0).wait()
    wait_rows(SUBSTEPS, (0,))
    south_f[0] = jnp.minimum(row_recv[SUBSTEPS, 0].astype(F32), 0.0)
    west_rim = rim_recv[SUBSTEPS, 0]
    for row in range(ROWS):
        faces = nat_a[pl.ds(row, LEV, stride=ROWS), :]
        west = dot(jnp.concatenate([faces.astype(BF), west_rim], axis=1), jnp.concatenate(
            [shift_m[:LON, LON:], ends_m[:LON, row * LON:(row + 1) * LON]], axis=0))
        west = jnp.minimum(west, 0.0)
        faces = jnp.maximum(faces, 0.0)
        east_f[row] = faces
        west_f[row] = west
        ends_f[row] = jnp.where(lane == LON - 1, faces, jnp.where(lane == 0, -west, 0.0))

    def inner(cells, new_cells):
        def one_row(row):
            centre = cells[row + 1]
            here = pl.ds(pl.multiple_of(row * LEV, LEV), LEV)
            new_cells[row + 1] = (
                centre + east_f[row] * (sides_s[here, :LON] - centre)
                + west_f[row] * (centre - sides_s[here, LON:])
                + north_f[row] * (cells[row + 2] - centre)
                + south_f[row] * (centre - cells[row]))

        loop(0, ROWS, one_row)

    def outer(slot, new_cells, store):
        rim_copy(slot, 0).wait()
        rim_copy(slot, 1).wait()
        wait_rows(slot, (0, 1))
        rims = jnp.concatenate([rim_recv[slot, 0], rim_recv[slot, 1]], axis=1)
        for row in range(0, ROWS, 2):
            ends = dot(rims, ends_m[:, row * LON:(row + 2) * LON])
            for i in range(2):
                new = new_cells[row + i + 1] + ends_f[row + i] * ends[:, i * LON:(i + 1) * LON]
                if row + i == 0:
                    new = new - south_f[0] * row_recv[slot, 0].astype(F32)
                if row + i == ROWS - 1:
                    new = new + north_f[ROWS - 1] * row_recv[slot, 1].astype(F32)
                store(row + i, new, new_cells)

    def into_natural(row, new, cells):
        out_nat[pl.ds(row, LEV, stride=ROWS), :] = new

    stores = [pltpu.make_async_copy(src, dst, store_sem.at[i]) for i, (src, dst) in enumerate(
        ((out_nat, out_hbm), (first, first_hbm), (second, second_hbm), (third, third_hbm)))]

    third_red, second_red, first_red = reds
    inner(cot_a, cot_b)
    third_red.step2()
    second_red.step2()
    outer(0, cot_b, keep)
    send_halo(1)
    first_red.step2()
    sides()
    inner(cot_b, cot_a)
    third_red.step3()
    outer(1, cot_a, keep)
    send_halo(2)
    sides()
    inner(cot_a, cot_b)
    second_red.step3()
    first_red.step3()
    third_red.step4()
    outer(2, cot_b, into_natural)
    stores[0].start()
    first_red.step4()
    second_red.step4()
    third_red.finish()

    def total(index):
        for (lo, count, _), red in zip(rounds, reds):
            if lo <= index < lo + count:
                return red.full[index - lo].astype(F32) * scale

    sum_third = total(4)
    for m in blocks:
        third[:, m] = sum_third[:, m].T
    stores[3].start()
    first_red.finish()
    sum_first = total(5)
    for m in blocks:
        first[m, :] = sum_first[:, m]
    stores[1].start()
    second_red.finish()
    for i, m in enumerate(blocks):
        second[m, :] = total(i)
    stores[2].start()
    for store in stores:
        store.wait()


def reduction_scratch(nb, plane_first):
    n1, n2 = (PLANE, DEPTH) if plane_first else (DEPTH, PLANE)
    width = HID * 4 // n1
    half, piece = (nb, 64, HID), (nb, 16, width)
    bufs = [
        pltpu.VMEM(half, BF), pltpu.VMEM(half, BF), pltpu.VMEM(half, F32), pltpu.VMEM(half, BF),
        pltpu.VMEM((n1 - 1,) + piece, BF), pltpu.VMEM((n2,) + piece, BF), pltpu.VMEM((nb, 128, HID), BF),
    ]
    dma = pltpu.SemaphoreType.DMA
    return bufs + [dma] * 10


def finish_kernel(*refs):
    ins, outs, held, load_sem, store_sem = refs[:4], refs[4:8], refs[8:12], refs[12], refs[13]
    moves = []
    for src, dst, buf in zip(ins, outs, held):
        size = min(src.shape[0], FINISH_ROWS * 128 // src.shape[1])
        for first in range(0, src.shape[0], size):
            rows = pl.ds(first, size)
            n = len(moves)
            moves.append((
                pltpu.make_async_copy(src.at[rows], buf.at[rows], load_sem.at[n]),
                pltpu.make_async_copy(buf.at[rows], dst.at[rows], store_sem.at[n])))
    for load, _ in moves:
        load.start()
    for load, store in moves:
        load.wait()
        store.start()
    for _, store in moves:
        store.wait()


def local(state, heat_cot, state_cot, courant_lon, courant_lat, w_first, w_second, w_third):
    levels, lat_rows, lon_cols = state.shape
    scale = 1.0 / math.sqrt(lat_rows * lon_cols * lax.axis_size("lat") * lax.axis_size("lon"))
    flat = (levels * lat_rows, lon_cols)
    hbm = pl.BlockSpec(memory_space=pl.ANY)
    dma = pltpu.SemaphoreType.DMA
    tile = (LEV, LON)
    bfs = lambda *shapes: [pltpu.VMEM(shape, BF) for shape in shapes]
    f32s = lambda *shapes: [pltpu.VMEM(shape, F32) for shape in shapes]
    grid = (ROWS,) + tile
    halo = (SUBSTEPS + 1, 2)
    scratch = [
        *f32s(flat, flat), *bfs(flat, flat), *f32s(flat), *bfs(flat, flat),
        *bfs((HID, LEV), (HID, HID), (LEV, HID), (LEV, HID), (HID, HID), (HID, LEV)),
        *f32s((LEV, COLS), (1, COLS)), *bfs((LEV, COLS), (HID, COLS)), *f32s((HID, COLS)),
        *bfs((HID, COLS), (2, HID, CHUNK)), *f32s((6, 128, 512)),
        *f32s((ROWS + 2,) + tile, (ROWS + 2,) + tile), *bfs(grid, grid), *f32s((COLS, 2 * LON)),
        *f32s(grid, grid, grid, (ROWS + 1,) + tile, grid),
        *bfs((2 * LON, 2 * LON), (2 * LON, COLS), (COLS, LON)),
        *f32s(flat, (HID, LEV), (HID, HID), (LEV, HID)),
        *bfs((SUBSTEPS + 1,) + tile, halo + tile, halo + tile, halo + tile),
        dma((8,)), dma((4,)), dma(halo), dma(halo), dma(halo), dma(halo),
    ]
    for _, count, plane_first in ROUNDS:
        scratch += reduction_scratch(count, plane_first)
    shapes = (flat, (HID, LEV), (HID, HID), (LEV, HID))
    results = tuple(jax.ShapeDtypeStruct(shape, F32) for shape in shapes)
    out = pl.pallas_call(
        functools.partial(kernel, scale, ROUNDS),
        out_shape=results,
        in_specs=[hbm] * 8,
        out_specs=(hbm,) * 4,
        scratch_shapes=scratch,
        compiler_params=pltpu.CompilerParams(
            collective_id=0, has_side_effects=True, vmem_limit_bytes=60 << 20),
    )(state.reshape(flat), heat_cot.reshape(flat), state_cot.reshape(flat),
      courant_lon.reshape(flat), courant_lat.reshape(flat), w_first, w_second, w_third)
    grid, first, second, third = pl.pallas_call(
        finish_kernel, out_shape=results, in_specs=[hbm] * 4, out_specs=(hbm,) * 4,
        scratch_shapes=[*f32s(*shapes), dma((16,)), dma((16,))],
        compiler_params=pltpu.CompilerParams(vmem_limit_bytes=60 << 20),
    )(*out)
    return grid.reshape(state.shape), first, second, third


def solution(mesh):
    split = P(None, "lat", "lon")
    return jax.shard_map(
        local, mesh=mesh, in_specs=(split,) * 5 + (P(),) * 3,
        out_specs=(split, P(), P(), P()), check_vma=False)
```

```python
import functools
import math

import jax
import jax.numpy as jnp
from jax import lax
from jax.experimental import pallas as pl
from jax.experimental.pallas import tpu as pltpu
from jax.sharding import PartitionSpec as P

EPSILON = 1e-05
SUBSTEPS = 3
MESH = pl.DeviceIdType.MESH
BF = jnp.bfloat16
F32 = jnp.float32
LEV = 128
HID = 512
ROWS = 16
LON = 128
COLS = ROWS * LON
CHUNK_ROWS = 4
CHUNK = CHUNK_ROWS * LON
CHUNKS = ROWS // CHUNK_ROWS
PLANE = 16
DEPTH = 8
ROUNDS = ((3, 2, False), (0, 3, True), (5, 1, False))
FINISH_ROWS = 512


def dot(a, b):
    return jnp.dot(a, b, preferred_element_type=F32)


def dot_last(a, b):
    return lax.dot_general(a, b, (((1,), (1,)), ((), ())), preferred_element_type=F32)


def silu_and_slope(pre):
    sigma = 0.5 * jnp.tanh(0.5 * pre) + 0.5
    act = pre * sigma
    return act, sigma + act * (1.0 - sigma)


def place():
    lat, lon = lax.axis_index("lat"), lax.axis_index("lon")
    core = lax.rem(lon, 2)
    depth = lax.rem(lax.div(lon, 2), DEPTH)
    plane = lat * 2 + lax.div(lon, 16)
    return lat, lon, core, depth, plane


def loop(lo, hi, body):
    lax.fori_loop(lo, hi, lambda k, carry: (body(k), carry)[1], 0)


class Reduction:
    def __init__(self, part, plane_first, bufs, sems):
        self.part = part
        self.send0, self.recv0, self.half, self.send1, self.recv1, self.recv2, self.full = bufs
        (self.s0, self.r0, self.s1, self.r1, self.s2, self.r2, self.s3, self.r3, self.s4, self.r4) = sems
        lat, lon, self.core, depth, plane = place()
        self.sibling = (lat, lon + 1 - 2 * self.core)
        x, y = lax.rem(lat, 4), lax.div(lat, 4) * 2 + lax.div(lon, 16)
        planes, depths = [], []
        for kx, ky in sorted(((a, b) for a in range(4) for b in range(4) if a or b),
                             key=lambda k: -min(k[0], 4 - k[0]) - min(k[1], 4 - k[1])):
            to_x, to_y = lax.rem(x + kx, 4), lax.rem(y + ky, 4)
            to_lat, to_part = lax.div(to_y, 2) * 4 + to_x, lax.rem(to_y, 2)
            planes.append((to_lat * 2 + to_part, (to_lat, to_part * 16 + lax.rem(lon, 16))))
        for k in sorted(range(1, DEPTH), key=lambda k: -min(k, DEPTH - k)):
            to = lax.rem(depth + k, DEPTH)
            depths.append((to, (lat, lax.div(lon, 16) * 16 + to * 2 + self.core)))
        groups = ((plane, planes), (depth, depths))
        (self.me1, self.peers1), (self.me2, self.peers2) = groups if plane_first else groups[::-1]
        self.across = 4 if plane_first else 2

    def piece(self, index, base=0):
        width = HID // self.across
        row = pl.multiple_of(base + lax.div(index, self.across) * 16, 16)
        lane = pl.multiple_of(lax.rem(index, self.across) * width, width)
        return (slice(None), pl.ds(row, 16), pl.ds(lane, width))

    def copy0(self):
        return pltpu.make_async_remote_copy(
            src_ref=self.send0, dst_ref=self.recv0, send_sem=self.s0, recv_sem=self.r0,
            device_id=self.sibling, device_id_type=MESH)

    def copies1(self):
        return [pltpu.make_async_remote_copy(
            src_ref=self.send1.at[self.piece(to)], dst_ref=self.recv1.at[n],
            send_sem=self.s1, recv_sem=self.r1,
            device_id=device, device_id_type=MESH) for n, (to, device) in enumerate(self.peers1)]

    def copies2(self):
        mine = self.recv2.at[self.me2]
        return [pltpu.make_async_remote_copy(
            src_ref=mine, dst_ref=mine, send_sem=self.s2, recv_sem=self.r2,
            device_id=device, device_id_type=MESH) for _, device in self.peers2]

    def copies3(self):
        mine = self.full.at[self.piece(self.me1, 64 * self.core)]
        return [pltpu.make_async_remote_copy(
            src_ref=mine, dst_ref=mine, send_sem=self.s3, recv_sem=self.r3,
            device_id=device, device_id_type=MESH) for _, device in self.peers1]

    def all_of(self, ref, send_sem, recv_sem):
        return pltpu.make_async_remote_copy(
            src_ref=ref, dst_ref=ref, send_sem=send_sem, recv_sem=recv_sem,
            device_id=self.sibling, device_id_type=MESH)

    def copy4(self):
        mine = self.full.at[:, pl.ds(pl.multiple_of(64 * self.core, 64), 64), :]
        return pltpu.make_async_remote_copy(
            src_ref=mine, dst_ref=mine, send_sem=self.s4, recv_sem=self.r4,
            device_id=self.sibling, device_id_type=MESH)

    def step0(self):
        other = pl.multiple_of(64 * (1 - self.core), 64)
        self.send0[...] = self.part[:, pl.ds(other, 64), :].astype(BF)
        self.copy0().start()

    def step1(self):
        self.copy0().wait()
        mine = pl.multiple_of(64 * self.core, 64)
        self.half[...] = self.part[:, pl.ds(mine, 64), :] + self.recv0[...].astype(F32)
        self.send1[...] = self.half[...].astype(BF)
        for copy in self.copies1():
            copy.start()

    def step2(self):
        self.all_of(self.recv1, self.s1, self.r1).wait()
        total = self.half[self.piece(self.me1)]
        for n in range(len(self.peers1)):
            total = total + self.recv1[n].astype(F32)
        self.recv2[self.me2] = total.astype(BF)
        for copy in self.copies2():
            copy.start()

    def step3(self):
        self.all_of(self.recv2.at[pl.ds(0, len(self.peers2))], self.s2, self.r2).wait()
        total = self.recv2[0].astype(F32)
        for n in range(1, len(self.peers2) + 1):
            total = total + self.recv2[n].astype(F32)
        self.full[self.piece(self.me1, 64 * self.core)] = total.astype(BF)
        for copy in self.copies3():
            copy.start()

    def step4(self):
        self.all_of(self.recv1, self.s3, self.r3).wait()
        self.copy4().start()

    def finish(self):
        self.copy4().wait()


def kernel(scale, rounds, state_hbm, heat_hbm, scot_hbm, clon_hbm, clat_hbm, w1_hbm, w2_hbm, w3_hbm,
           out_hbm, first_hbm, second_hbm, third_hbm,
           nat_a, nat_b, state, heat, scot, clon, clat, w1, w2, w3, w1t, w2t, w3t,
           normed_s, inv_s, inputs_s, act1_s, slope1_s, back2_s, act2_s, part,
           cot_a, cot_b, high_s, low_s, sides_s, east_f, west_f, north_f, south_f, ends_f,
           shift_m, ends_m, pack_m, out_nat, first, second, third,
           rim_send, rim_recv, row_send, row_recv,
           load_sem, store_sem, rim_ss, rim_rs, row_ss, row_rs,
           *rest):
    lat, lon, core, depth, plane = place()
    lats, lons = lax.axis_size("lat"), lax.axis_size("lon")
    west_id = (lat, lax.rem(lon + lons - 1, lons))
    east_id = (lat, lax.rem(lon + 1, lons))
    up, down = lat < lats - 1, lat > 0
    reds = []
    for n, (lo, count, plane_first) in enumerate(rounds):
        own = rest[17 * n:17 * (n + 1)]
        reds.append(Reduction(part.at[pl.ds(lo, count)], plane_first, own[:7], own[7:]))
    early = reds[:-1]

    barrier = pltpu.get_barrier_semaphore()

    def greet(device):
        pl.semaphore_signal(barrier, inc=1, device_id=device, device_id_type=MESH)

    for _, device in reds[0].peers1 + reds[0].peers2:
        greet(device)
    greet(reds[0].sibling)
    greet(west_id)
    greet(east_id)

    loads = [pltpu.make_async_copy(src, dst, load_sem.at[i]) for i, (src, dst) in
             enumerate(((state_hbm, state), (w1_hbm, w1), (w2_hbm, w2), (w3_hbm, w3), (heat_hbm, heat),
                        (clon_hbm, clon), (clat_hbm, clat), (scot_hbm, scot)))]
    for load in loads:
        load.start()

    down_i = lax.broadcasted_iota(jnp.int32, (LEV, LON), 0)
    lane = lax.broadcasted_iota(jnp.int32, (LEV, LON), 1)
    for half in range(2):
        shift_m[half * LON:(half + 1) * LON, :LON] = (down_i == lane + 1).astype(BF)
        shift_m[half * LON:(half + 1) * LON, LON:] = (down_i + 1 == lane).astype(BF)
    for row in range(ROWS):
        cols = slice(row * LON, (row + 1) * LON)
        ends_m[:LON, cols] = jnp.where((down_i == 2 * row) & (lane == 0), 1.0, 0.0).astype(BF)
        ends_m[LON:, cols] = jnp.where(
            (down_i == 2 * row + 1) & (lane == LON - 1), 1.0, 0.0).astype(BF)
        pack_m[cols, :] = jnp.where(
            ((down_i == LON - 1) & (lane == 2 * row)) | ((down_i == 0) & (lane == 2 * row + 1)),
            1.0, 0.0).astype(BF)
    cot_a[0] = jnp.zeros((LEV, LON), F32)
    cot_b[0] = jnp.zeros((LEV, LON), F32)
    cot_a[ROWS + 1] = jnp.zeros((LEV, LON), F32)
    cot_b[ROWS + 1] = jnp.zeros((LEV, LON), F32)

    @pl.when(jnp.logical_not(down))
    def _():
        for slot in range(SUBSTEPS + 1):
            row_recv[slot, 0] = jnp.zeros((LEV, LON), BF)

    @pl.when(jnp.logical_not(up))
    def _():
        for slot in range(SUBSTEPS):
            row_recv[slot, 1] = jnp.zeros((LEV, LON), BF)

    for load in loads[:5]:
        load.wait()
    nat_a[...] = state[...].astype(F32)
    nat_b[...] = heat[...].astype(F32)
    w1t[...] = w1[...].T
    w2t[...] = w2[...].T
    w3t[...] = w3[...].T

    def rows_of(ref, first):
        return jnp.concatenate(
            [ref[pl.ds(first + i, LEV, stride=ROWS), :] for i in range(CHUNK_ROWS)], axis=1)

    blocks = [slice(128 * m, 128 * (m + 1)) for m in range(4)]

    def add_blocks(index, terms, new):
        for m in blocks:
            part[index, :, m] = terms[m, :] if new else part[index, :, m] + terms[m, :]

    def forward(chunk):
        cols = slice(chunk * CHUNK, (chunk + 1) * CHUNK)
        values = rows_of(nat_a, chunk * CHUNK_ROWS)
        inverse = lax.rsqrt(jnp.mean(values * values, axis=0, keepdims=True) + EPSILON)
        normed = values * inverse
        inputs = normed.astype(BF)
        normed_s[:, cols] = normed
        inv_s[:, cols] = inverse
        inputs_s[:, cols] = inputs
        cot = rows_of(nat_b, chunk * CHUNK_ROWS).astype(BF)
        act, slope = silu_and_slope(dot(w1[...], inputs))
        act1_s[:, cols] = act.astype(BF)
        slope1_s[:, cols] = slope
        act, slope = silu_and_slope(dot(w2[...], act1_s[:, cols]))
        act2_s[chunk % 2] = act.astype(BF)
        back2_s[:, cols] = (dot(w3t[...], cot) * slope).astype(BF)
        add_blocks(4, dot_last(act2_s[chunk % 2], cot), chunk == 0)
        terms = dot_last(back2_s[:, cols], act1_s[:, cols]).reshape(4, 128, HID)
        part[:4] = terms if chunk == 0 else part[:4] + terms

    for chunk in range(CHUNKS):
        forward(chunk)
    pl.semaphore_wait(barrier, (PLANE - 1) + (DEPTH - 1) + 3)
    for red in early:
        red.step0()

    def rim_copy(slot, way):
        return pltpu.make_async_remote_copy(
            src_ref=rim_send.at[slot], dst_ref=rim_recv.at[slot, way],
            send_sem=rim_ss.at[slot, way], recv_sem=rim_rs.at[slot, way],
            device_id=(east_id, west_id)[way], device_id_type=MESH)

    def row_copy(slot, way):
        return pltpu.make_async_remote_copy(
            src_ref=row_send.at[slot, way], dst_ref=row_recv.at[slot, way],
            send_sem=row_ss.at[slot, way], recv_sem=row_rs.at[slot, way],
            device_id=(jnp.clip(lat + (1, -1)[way], 0, lats - 1), lon), device_id_type=MESH)

    def send_rows(slot, ways):
        for way in ways:
            pl.when((up, down)[way])(lambda: row_copy(slot, way).start())

    def wait_rows(slot, ways):
        for way in ways:
            pl.when((up, down)[way])(lambda: row_copy(slot, way).wait_send())
            pl.when((down, up)[way])(lambda: row_copy(slot, way).wait_recv())

    def backward(chunk):
        cols = slice(chunk * CHUNK, (chunk + 1) * CHUNK)
        back = (dot(w2t[...], back2_s[:, cols]) * slope1_s[:, cols]).astype(BF)
        act2_s[chunk % 2] = back
        add_blocks(5, dot_last(back, inputs_s[:, cols]), chunk == 0)
        input_cot = dot(w1t[...], act2_s[chunk % 2])
        normed = normed_s[:, cols]
        state_part = inv_s[:, cols] * (
            input_cot - normed * jnp.mean(input_cot * normed, axis=0, keepdims=True))
        for i in range(CHUNK_ROWS):
            row = chunk * CHUNK_ROWS + i
            keep(row, state_part[:, i * LON:(i + 1) * LON] + scot[pl.ds(row, LEV, stride=ROWS), :],
                 cot_a)

    def keep(row, new, cells):
        cells[row + 1] = new
        high = new.astype(BF)
        high_s[row] = high
        low_s[row] = (new - high.astype(F32)).astype(BF)

    def packed():
        return sum(dot(jnp.concatenate([high_s[row], high_s[row + 1]], axis=1),
                       pack_m[row * LON:(row + 2) * LON, :]) for row in range(0, ROWS, 2)).astype(BF)

    loads[5].wait()
    loads[6].wait()
    nat_a[...] = clon[...].astype(F32)
    nat_b[...] = clat[...].astype(F32)
    row_send[SUBSTEPS, 0] = nat_b[pl.ds(ROWS - 1, LEV, stride=ROWS), :].astype(BF)
    send_rows(SUBSTEPS, (0,))
    faces_pairs = [jnp.concatenate(
        [nat_a[pl.ds(row + i, LEV, stride=ROWS), :].astype(BF) for i in range(2)], axis=1)
        for row in range(0, ROWS, 2)]
    rim_send[SUBSTEPS] = sum(dot(pair, pack_m[2 * i * LON:2 * (i + 1) * LON, :])
                             for i, pair in enumerate(faces_pairs)).astype(BF)
    rim_copy(SUBSTEPS, 0).start()
    loads[7].wait()
    backward(0)
    for red in early:
        red.step1()
    for chunk in range(1, CHUNKS):
        backward(chunk)
    reds[-1].step0()

    def send_halo(slot):
        row_send[slot, 0] = high_s[ROWS - 1]
        row_send[slot, 1] = high_s[0]
        send_rows(slot, (0, 1))
        rim_send[slot] = packed()
        rim_copy(slot, 0).start()
        rim_copy(slot, 1).start()

    send_halo(0)

    def sides():
        sides_s[...] = dot(jnp.concatenate(
            [high_s[...].reshape(COLS, LON), low_s[...].reshape(COLS, LON)], axis=1), shift_m[...])

    sides()

    def split_lat(row):
        ahead = nat_b[pl.ds(row, LEV, stride=ROWS), :]
        north_f[row] = jnp.maximum(ahead, 0.0)
        south_f[row + 1] = jnp.minimum(ahead, 0.0)

    loop(0, ROWS, split_lat)
    reds[-1].step1()
    rim_copy(SUBSTEPS, 0).wait()
    wait_rows(SUBSTEPS, (0,))
    south_f[0] = jnp.minimum(row_recv[SUBSTEPS, 0].astype(F32), 0.0)
    west_rim = rim_recv[SUBSTEPS, 0]
    for row in range(ROWS):
        faces = nat_a[pl.ds(row, LEV, stride=ROWS), :]
        west = dot(jnp.concatenate([faces.astype(BF), west_rim], axis=1), jnp.concatenate(
            [shift_m[:LON, LON:], ends_m[:LON, row * LON:(row + 1) * LON]], axis=0))
        west = jnp.minimum(west, 0.0)
        faces = jnp.maximum(faces, 0.0)
        east_f[row] = faces
        west_f[row] = west
        ends_f[row] = jnp.where(lane == LON - 1, faces, jnp.where(lane == 0, -west, 0.0))

    def inner(cells, new_cells):
        def one_row(row):
            centre = cells[row + 1]
            here = pl.ds(pl.multiple_of(row * LEV, LEV), LEV)
            new_cells[row + 1] = (
                centre + east_f[row] * (sides_s[here, :LON] - centre)
                + west_f[row] * (centre - sides_s[here, LON:])
                + north_f[row] * (cells[row + 2] - centre)
                + south_f[row] * (centre - cells[row]))

        loop(0, ROWS, one_row)

    def outer(slot, new_cells, store):
        rim_copy(slot, 0).wait()
        rim_copy(slot, 1).wait()
        wait_rows(slot, (0, 1))
        rims = jnp.concatenate([rim_recv[slot, 0], rim_recv[slot, 1]], axis=1)
        for row in range(0, ROWS, 2):
            ends = dot(rims, ends_m[:, row * LON:(row + 2) * LON])
            for i in range(2):
                new = new_cells[row + i + 1] + ends_f[row + i] * ends[:, i * LON:(i + 1) * LON]
                if row + i == 0:
                    new = new - south_f[0] * row_recv[slot, 0].astype(F32)
                if row + i == ROWS - 1:
                    new = new + north_f[ROWS - 1] * row_recv[slot, 1].astype(F32)
                store(row + i, new, new_cells)

    def into_natural(row, new, cells):
        out_nat[pl.ds(row, LEV, stride=ROWS), :] = new

    stores = [pltpu.make_async_copy(src, dst, store_sem.at[i]) for i, (src, dst) in enumerate(
        ((out_nat, out_hbm), (first, first_hbm), (second, second_hbm), (third, third_hbm)))]

    third_red, second_red, first_red = reds
    inner(cot_a, cot_b)
    third_red.step2()
    second_red.step2()
    outer(0, cot_b, keep)
    send_halo(1)
    first_red.step2()
    sides()
    inner(cot_b, cot_a)
    third_red.step3()
    outer(1, cot_a, keep)
    send_halo(2)
    sides()
    inner(cot_a, cot_b)
    second_red.step3()
    first_red.step3()
    third_red.step4()
    outer(2, cot_b, into_natural)
    stores[0].start()
    first_red.step4()
    second_red.step4()
    third_red.finish()

    def total(index):
        for (lo, count, _), red in zip(rounds, reds):
            if lo <= index < lo + count:
                return red.full[index - lo].astype(F32) * scale

    sum_third = total(4)
    for m in blocks:
        third[:, m] = sum_third[:, m].T
    stores[3].start()
    first_red.finish()
    sum_first = total(5)
    for m in blocks:
        first[m, :] = sum_first[:, m]
    stores[1].start()
    second_red.finish()
    for i, m in enumerate(blocks):
        second[m, :] = total(i)
    stores[2].start()
    for store in stores:
        store.wait()


def reduction_scratch(nb, plane_first):
    n1, n2 = (PLANE, DEPTH) if plane_first else (DEPTH, PLANE)
    width = HID * 4 // n1
    half, piece = (nb, 64, HID), (nb, 16, width)
    bufs = [
        pltpu.VMEM(half, BF), pltpu.VMEM(half, BF), pltpu.VMEM(half, F32), pltpu.VMEM(half, BF),
        pltpu.VMEM((n1 - 1,) + piece, BF), pltpu.VMEM((n2,) + piece, BF), pltpu.VMEM((nb, 128, HID), BF),
    ]
    dma = pltpu.SemaphoreType.DMA
    return bufs + [dma] * 10


def finish_kernel(*refs):
    ins, outs, held, load_sem, store_sem = refs[:4], refs[4:8], refs[8:12], refs[12], refs[13]
    moves = []
    for src, dst, buf in zip(ins, outs, held):
        size = min(src.shape[0], FINISH_ROWS * 128 // src.shape[1])
        for first in range(0, src.shape[0], size):
            rows = pl.ds(first, size)
            n = len(moves)
            moves.append((
                pltpu.make_async_copy(src.at[rows], buf.at[rows], load_sem.at[n]),
                pltpu.make_async_copy(buf.at[rows], dst.at[rows], store_sem.at[n])))
    for load, _ in moves:
        load.start()
    for load, store in moves:
        load.wait()
        store.start()
    for _, store in moves:
        store.wait()


def local(state, heat_cot, state_cot, courant_lon, courant_lat, w_first, w_second, w_third):
    levels, lat_rows, lon_cols = state.shape
    scale = 1.0 / math.sqrt(lat_rows * lon_cols * lax.axis_size("lat") * lax.axis_size("lon"))
    flat = (levels * lat_rows, lon_cols)
    hbm = pl.BlockSpec(memory_space=pl.ANY)
    dma = pltpu.SemaphoreType.DMA
    tile = (LEV, LON)
    bfs = lambda *shapes: [pltpu.VMEM(shape, BF) for shape in shapes]
    f32s = lambda *shapes: [pltpu.VMEM(shape, F32) for shape in shapes]
    grid = (ROWS,) + tile
    halo = (SUBSTEPS + 1, 2)
    scratch = [
        *f32s(flat, flat), *bfs(flat, flat), *f32s(flat), *bfs(flat, flat),
        *bfs((HID, LEV), (HID, HID), (LEV, HID), (LEV, HID), (HID, HID), (HID, LEV)),
        *f32s((LEV, COLS), (1, COLS)), *bfs((LEV, COLS), (HID, COLS)), *f32s((HID, COLS)),
        *bfs((HID, COLS), (2, HID, CHUNK)), *f32s((6, 128, 512)),
        *f32s((ROWS + 2,) + tile, (ROWS + 2,) + tile), *bfs(grid, grid), *f32s((COLS, 2 * LON)),
        *f32s(grid, grid, grid, (ROWS + 1,) + tile, grid),
        *bfs((2 * LON, 2 * LON), (2 * LON, COLS), (COLS, LON)),
        *f32s(flat, (HID, LEV), (HID, HID), (LEV, HID)),
        *bfs((SUBSTEPS + 1,) + tile, halo + tile, halo + tile, halo + tile),
        dma((8,)), dma((4,)), dma(halo), dma(halo), dma(halo), dma(halo),
    ]
    for _, count, plane_first in ROUNDS:
        scratch += reduction_scratch(count, plane_first)
    shapes = (flat, (HID, LEV), (HID, HID), (LEV, HID))
    results = tuple(jax.ShapeDtypeStruct(shape, F32) for shape in shapes)
    out = pl.pallas_call(
        functools.partial(kernel, scale, ROUNDS),
        out_shape=results,
        in_specs=[hbm] * 8,
        out_specs=(hbm,) * 4,
        scratch_shapes=scratch,
        compiler_params=pltpu.CompilerParams(
            collective_id=0, has_side_effects=True, vmem_limit_bytes=60 << 20),
    )(state.reshape(flat), heat_cot.reshape(flat), state_cot.reshape(flat),
      courant_lon.reshape(flat), courant_lat.reshape(flat), w_first, w_second, w_third)
    grid, first, second, third = pl.pallas_call(
        finish_kernel, out_shape=results, in_specs=[hbm] * 4, out_specs=(hbm,) * 4,
        scratch_shapes=[*f32s(*shapes), dma((16,)), dma((16,))],
        compiler_params=pltpu.CompilerParams(vmem_limit_bytes=60 << 20),
    )(*out)
    return grid.reshape(state.shape), first, second, third


def solution(mesh):
    split = P(None, "lat", "lon")
    return jax.shard_map(
        local, mesh=mesh, in_specs=(split,) * 5 + (P(),) * 3,
        out_specs=(split, P(), P(), P()), check_vma=False)
```
